768 devices in a mesh: grp: 6 (over z_lo, core), blk: 128 (over x, y, z_hi).
Axes of the slice: x: 4, y: 8, z: 12 (z_hi: 4, z_lo: 3; z = z_hi * 3 + z_lo), core: 2. Of those that a mesh axis runs over, the one named last changes fastest.
Arguments:
- query_hidden: bfloat16 [98304, 2048], P(('grp', 'blk')), as said below
- query_proj: bfloat16 [2048, 512], replicated, may hold values from -0.125 to 0.125
- item_embed: bfloat16 [6144, 512], P(('grp', 'blk')), may hold values from -6 to 6
- positive: int32 [98304], P(('grp', 'blk')), may hold values from 0 to 1023
- hard_ids: int32 [98304, 8], P(('grp', 'blk')), may hold values from 0 to 1023
Outputs:
- item_grad: float32 [6144, 512], P(('grp', 'blk'))
- weight_update: float32 [2048, 512], P('blk')
The draws below stay inside these ranges and needn't reach their ends.
Inputs may be any that keep to these rules, and one draw needn't show every extreme that they name: `positive`: index of the query's positive item among the 1024 items of its group. `hard_ids`: indices among the 1024 items of the query's group; some items are named far more often than others. `query_hidden`: hidden activations.
All inputs are finite; a program needn't handle non-finite values.
Results may differ from the reference program's by a relative error of at most 0.0053.
Values may be sent and summed in bfloat16 or wider, within the bound.
A program may use at most 64 MiB of HBM per device.

```python
import math
import jax
import jax.numpy as jnp
import numpy as np
from jax import lax

EMB = 512
HID = 2048
HARD = 8
GROUP_QUERIES = 16384
GROUP_ITEMS = 1024
QUERIES = 98304
ITEMS = 6144
N_GRP = 6


def draw_query_hidden(key, part):
    key = jax.random.fold_in(key, 7)
    noise_key, rough_key = jax.random.split(key, 2)
    column = jnp.arange(HID, dtype=jnp.float32) / (HID - 1)
    rough_scale = jnp.exp(jax.random.uniform(rough_key, (HID,), minval=0.0, maxval=0.7))
    noise_draw = jnp.clip(jax.random.normal(noise_key, (QUERIES, HID), dtype=jnp.float32), -6.0, 6.0)
    rise_scale = 1.0 + 2.0 * column
    return (noise_draw * rise_scale * rough_scale).astype(jnp.bfloat16)


def place_ends(entries, rng, smallest, top_value):
    extent = entries.shape
    spot = [jax.random.randint(jax.random.fold_in(rng, axis), (), 0, extent[axis]) for axis in range(len(extent))]
    entries = entries.at[tuple(spot)].set(smallest)
    longest = extent.index(max(extent))
    spot[longest] = (spot[longest] + 1) % extent[longest]
    return entries.at[tuple(spot)].set(top_value)


def levels(own_key, extent, cuts, smallest, top_value):
    loudness, own = 1.0, jax.random.fold_in(own_key, 6)
    for axis_at, parts in cuts:
        draws = jnp.exp(jax.random.uniform(jax.random.fold_in(own, axis_at), (parts,), jnp.float32, smallest / len(cuts), top_value / len(cuts)))
        loudness = loudness * jnp.repeat(draws, extent[axis_at] // parts).reshape([-1 if axis == axis_at else 1 for axis in range(len(extent))])
    return loudness


def rank_bounds(number_of, skew):
    weights = [(1 << 20) // math.isqrt(grade ** skew) + 1 for grade in range(1, number_of + 1)]
    deviation = 1 + sum(weights) // (1 << 30)
    return np.cumsum(np.array([max(1, weight // deviation) for weight in weights]))


def ranked(own_key, extent, amount, slope):
    table = rank_bounds(amount, slope)
    lot = jax.random.randint(jax.random.fold_in(own_key, 1), extent, 0, int(table[amount - 1]))
    rank = jnp.searchsorted(jnp.asarray(table, jnp.int32), lot, side="right")
    return jax.random.permutation(jax.random.fold_in(own_key, 2), amount)[rank].astype(jnp.int32)


def centred(rng, dims, deviation, limit, shards=(), kind=jnp.bfloat16):
    array = deviation * jax.random.normal(rng, dims, jnp.float32)
    if shards:
        array = array * levels(rng, dims, shards, -0.22, 0.18)
    return jnp.clip(array, -limit, limit).astype(kind)


def setup_inputs(seed: int = 0) -> dict:
    splits = jax.random.split(jax.random.key(seed), 6)
    return {
        "query_hidden": draw_query_hidden(jax.random.fold_in(splits[5], 71), 0),
        "query_proj": centred(splits[1], (HID, EMB), HID ** -0.5, 0.125),
        "item_embed": centred(splits[2], (ITEMS, EMB), 1.0, 6.0, ((0, 768),)),
        "positive": place_ends(jax.random.randint(splits[3], (QUERIES,), 0, GROUP_ITEMS), jax.random.fold_in(splits[3], 1), 0, GROUP_ITEMS - 1).astype(jnp.int32),
        "hard_ids": place_ends(ranked(splits[4], (QUERIES, HARD), GROUP_ITEMS, 2), jax.random.fold_in(splits[4], 3), 0, GROUP_ITEMS - 1).astype(jnp.int32),
    }


INV_TAU = 50.0
EPSILON = 1e-06

def normalize_rows(values):
    inverse = lax.rsqrt(lax.optimization_barrier(jnp.sum(values * values, axis=-1, keepdims=True)) + EPSILON)
    return (values * inverse, inverse)

def reference(query_hidden, query_proj, item_embed, positive, hard_ids):
    hidden_groups = query_hidden.reshape(N_GRP, GROUP_QUERIES, HID)
    item_groups = item_embed.reshape(N_GRP, GROUP_ITEMS, EMB)
    positive_groups = positive.reshape(N_GRP, GROUP_QUERIES)
    hard_groups = hard_ids.reshape(N_GRP, GROUP_QUERIES, HARD)

    def one_group(running, group_data):
        hidden, item_rows, positive_ids, hard_rows = group_data
        query_raw = jnp.dot(hidden, query_proj, preferred_element_type=jnp.float32)
        query_dir, query_inv = normalize_rows(query_raw)
        query_unit = query_dir.astype(jnp.bfloat16)
        item_dir, item_inv = normalize_rows(item_rows.astype(jnp.float32))
        item_unit = item_dir.astype(jnp.bfloat16)
        scores = jnp.dot(query_unit, item_unit.T, preferred_element_type=jnp.float32) * INV_TAU
        log_total = jnp.log(lax.optimization_barrier(jnp.sum(jnp.exp(scores), axis=1, keepdims=True)))
        soft = jnp.exp(scores - log_total)
        pos_score = jnp.take_along_axis(scores, positive_ids[:, None], axis=1)
        hard_score = jnp.take_along_axis(scores, hard_rows, axis=1)
        hard_weight = jax.nn.sigmoid(hard_score - pos_score)
        columns = lax.broadcasted_iota(jnp.int32, scores.shape, 1)
        extra = jnp.float32(1.0) + lax.optimization_barrier(jnp.sum(hard_weight, axis=1, keepdims=True))
        grad_rows = soft - jnp.where(columns == positive_ids[:, None], extra, jnp.zeros_like(soft))
        row_index = lax.broadcasted_iota(jnp.int32, hard_rows.shape, 0)
        grad_rows = grad_rows.at[row_index, hard_rows].add(hard_weight)
        score_grad = (grad_rows * INV_TAU).astype(jnp.bfloat16)
        query_grad = jnp.dot(score_grad, item_unit, preferred_element_type=jnp.float32)
        raw_grad = (query_inv * (query_grad - query_dir * lax.optimization_barrier(jnp.sum(query_dir * query_grad, axis=-1, keepdims=True)))).astype(jnp.bfloat16)
        unit_grad = jnp.dot(score_grad.T, query_unit, preferred_element_type=jnp.float32)
        item_grad = item_inv * (unit_grad - item_dir * lax.optimization_barrier(jnp.sum(item_dir * unit_grad, axis=-1, keepdims=True)))
        running = running + jnp.dot(hidden.T, raw_grad, preferred_element_type=jnp.float32)
        return (running, item_grad)
    weight_sum, item_grads = lax.scan(one_group, jnp.zeros((HID, EMB), jnp.float32), (hidden_groups, item_groups, positive_groups, hard_groups))
    weight_update = weight_sum * lax.rsqrt(jnp.mean(weight_sum * weight_sum) + EPSILON)
    return (item_grads.reshape(ITEMS, EMB), weight_update)
```

```python
import functools

import jax
import jax.numpy as jnp
from jax import lax
from jax.experimental import pallas as pl
from jax.experimental.pallas import tpu as pltpu
from jax.sharding import PartitionSpec as P

MESH = pl.DeviceIdType.MESH
F32, BF16 = jnp.float32, jnp.bfloat16
INV_TAU = 50.0
EPSILON = 1e-06

NX, NY, NH, NL, NC = 4, 8, 4, 3, 2


def mod(value, size):
    return lax.rem(value + size, size)


def kernel(sizes, hid_hbm, proj_hbm, item_ref, pos_ref, hard_ref, ig_ref, wu_ref, s):
    nx, ny, nh, nl, nc = sizes
    q, hid = hid_hbm.shape
    emb = proj_hbm.shape[1]
    ipd = item_ref.shape[0]
    half = emb // 2
    wpd = wu_ref.shape[0]
    yr, ic = nh * ipd, ny * nh * ipd
    wyr, wc = nh * wpd, ny * nh * wpd

    grp, blk = lax.axis_index("grp"), lax.axis_index("blk")
    x, y, h = blk // (ny * nh), (blk // nh) % ny, blk % nh
    l, c = grp // nc, grp % nc

    def at(dx=0, dy=0, dh=0, dl=0, dc=0):
        place = (mod(x + dx, nx) * ny + mod(y + dy, ny)) * nh + mod(h + dh, nh)
        return (mod(l + dl, nl) * nc + mod(c + dc, nc), place)

    started = []

    def send(src, dst, device):
        i = len(started)
        copy = pltpu.make_async_remote_copy(
            src_ref=src,
            dst_ref=dst,
            send_sem=s["send"].at[i],
            recv_sem=s["recv"].at[i],
            device_id=device,
            device_id_type=MESH,
        )
        copy.start()
        started.append(copy)
        return copy

    partners = [at(dx=d) for d in range(1, nx)]
    partners += [at(dy=d) for d in range(1, ny)]
    partners += [at(dh=d) for d in range(1, nh)]
    others = [(dl, dc) for dl in range(nl) for dc in range(nc) if (dl, dc) != (0, 0)]
    partners += [at(dl=dl, dc=dc) for dl, dc in others]
    left, right, twin = at(dx=-1), at(dx=1), at(dc=1)

    barrier = pltpu.get_barrier_semaphore()
    for device in partners:
        pl.semaphore_signal(barrier, inc=1, device_id=device, device_id_type=MESH)
    load_proj = pltpu.make_async_copy(proj_hbm, s["proj"], s["local"].at[0])
    load_proj.start()
    load_hid = pltpu.make_async_copy(hid_hbm, s["h2"].at[pl.ds(0, q)], s["local"].at[1])
    load_hid.start()

    item = item_ref[...].astype(F32)
    item_inv = lax.rsqrt(jnp.sum(item * item, axis=-1, keepdims=True) + EPSILON)
    item_dir = item * item_inv
    s["hbuf"][0] = jnp.concatenate([item_dir[:, :half], item_dir[:, half:]], axis=0).astype(BF16)

    pl.semaphore_wait(barrier, len(partners))
    got_h = [send(s["hbuf"].at[0], s["hbuf"].at[d], at(dh=d)) for d in range(1, nh)]
    got_hid = send(hid_hbm, s["h2"].at[pl.ds(q, q)], twin)

    load_hid.wait()
    load_proj.wait()
    raw = jnp.dot(s["h2"][pl.ds(0, q), :], s["proj"][...], preferred_element_type=F32)
    query_inv = lax.rsqrt(jnp.sum(raw * raw, axis=-1, keepdims=True) + EPSILON)
    s["qd"][...] = raw * query_inv
    s["qu"][...] = s["qd"][...].astype(BF16)
    s["qinv"][...] = jnp.broadcast_to(query_inv, s["qinv"].shape)

    for copy in got_h:
        copy.wait_recv()
    for d in range(nh):
        block = s["hbuf"][d].astype(F32)
        s["hrow"][pl.ds(d * ipd, ipd), :] = jnp.concatenate([block[:ipd], block[ipd:]], axis=1)
    g = s["g"]
    g[0, pl.ds(0, yr), :] = s["hrow"][...].astype(BF16)

    def piece(slot, d):
        return g.at[slot, pl.ds(d * yr, yr)]

    got_y = {d: send(piece(0, 0), piece(0, d), at(dy=d)) for d in range(1, ny)}
    from_left, from_right, from_far = {}, {}, {}

    def pass_on(d):
        from_left[d].wait_recv()
        if d % 2 == 0:
            from_far[d] = send(piece(1, d), piece(2, d), right)
        from_right[d].wait_recv()
        if d % 2 == 1:
            from_far[d] = send(piece(3, d), piece(2, d), left)

    for d in range(ny):
        if d:
            got_y[d].wait_recv()
        from_left[d] = send(piece(0, d), piece(1, d), right)
        from_right[d] = send(piece(0, d), piece(3, d), left)
        if d == 0:
            s["h2t"][:, pl.ds(0, q)] = s["h2"][pl.ds(0, q), :].T
        if d >= 2:
            pass_on(d - 2)
    for d in range(max(ny - 2, 0), ny):
        pass_on(d)

    def column(ids):
        i, p = ids % ipd, ids // ipd
        hh, p = p % nh, p // nh
        yy, xx = p % ny, p // ny
        return ((mod(x - xx, nx) * ny + mod(y - yy, ny)) * nh + mod(h - hh, nh)) * ipd + i

    pos = column(jnp.broadcast_to(pos_ref[...], (q, q)).T[:, :1])
    ids = [pos] + [
        column(jnp.broadcast_to(hard_ref[k : k + 1, :], (q, q)).T[:, :1])
        for k in range(hard_ref.shape[0])
    ]
    lane = lax.broadcasted_iota(jnp.int32, (q, ic), 1)
    total = jnp.zeros((q, 1), F32)
    picks = [jnp.zeros((q, 1), F32) for _ in ids]
    for slot in (0, 1, 3, 2):
        if slot == 2:
            for d in range(ny):
                from_far[d].wait_recv()
        scores = lax.dot_general(
            s["qu"][...], g[slot], (((1,), (1,)), ((), ())), preferred_element_type=F32
        )
        e = jnp.exp(scores * INV_TAU)
        s["e"][slot] = e
        total = total + jnp.sum(e, axis=1, keepdims=True)
        for k, column_of in enumerate(ids):
            hit = lane == column_of - slot * ic
            picks[k] = picks[k] + jnp.sum(jnp.where(hit, e, 0.0), axis=1, keepdims=True)

    weights = [pick / (pick + picks[0]) for pick in picks[1:]]
    extra = 1.0 + functools.reduce(jnp.add, weights)
    inverse = 1.0 / total
    query_grad = jnp.zeros((q, emb), F32)
    for slot in range(nx):
        grad = s["e"][slot] * inverse
        for k, column_of in enumerate(ids):
            hit = lane == column_of - slot * ic
            grad = grad + jnp.where(hit, -extra if k == 0 else weights[k - 1], 0.0)
        s["sg"][slot] = (grad * INV_TAU).astype(BF16)
        query_grad = query_grad + jnp.dot(s["sg"][slot], g[slot], preferred_element_type=F32)

    query_dir = s["qd"][...]
    inner = jnp.sum(query_dir * query_grad, axis=-1, keepdims=True)
    raw_grad = (s["qinv"][:, :1] * (query_grad - query_dir * inner)).astype(BF16)
    s["raw"][0] = raw_grad[:, :half]
    s["raw"][1] = raw_grad[:, half:]
    got_raw = send(s["raw"].at[mod(c + 1, nc)], s["raw2"].at[pl.ds(q, q)], twin)
    s["raw2"][pl.ds(0, q), :] = s["raw"][c]

    got_hid.wait_recv()
    s["h2t"][:, pl.ds(q, q)] = s["h2"][pl.ds(q, q), :].T

    def parts(name, term, rows):
        n = rows // 2
        a, b = pl.ds(0, n), pl.ds(n, n)
        own, far, to_right, to_left, in_a, in_b, in_left, in_right = (
            s[name + "_" + key] for key in ("own", "far", "tr", "tl", "ia", "ib", "il", "ir")
        )
        keep_a, keep_b = s[name + "_ka"], s[name + "_kb"]
        out = {}

        def fill():
            far[...] = term(2).astype(BF16)
            value = term(3)
            keep_a[...] = value[:n]
            to_right[b, :] = value[n:].astype(BF16)
            value = term(1)
            keep_b[...] = value[n:]
            to_left[a, :] = value[:n].astype(BF16)
            own[...] = term(0)

        def first():
            out["a"] = send(far.at[a], in_a, right)
            out["b"] = send(far.at[b], in_b, left)
            out["rb"] = send(to_right.at[b], in_left.at[b], right)
            out["la"] = send(to_left.at[a], in_right.at[a], left)

        def second():
            out["a"].wait_recv()
            to_right[a, :] = (keep_a[...] + in_a[...].astype(F32)).astype(BF16)
            out["ra"] = send(to_right.at[a], in_left.at[a], right)
            out["b"].wait_recv()
            to_left[b, :] = (keep_b[...] + in_b[...].astype(F32)).astype(BF16)
            out["lb"] = send(to_left.at[b], in_right.at[b], left)

        def last():
            for key in ("rb", "la", "ra", "lb"):
                out[key].wait_recv()
            value = own[...] + in_left[...].astype(F32) + in_right[...].astype(F32)
            own[...] = value
            s[name + "_sum"][...] = value.astype(BF16)

        return fill, first, second, last

    def unit_term(slot):
        return lax.dot_general(
            s["sg"][slot], s["qu"][...], (((0,), (0,)), ((), ())), preferred_element_type=F32
        )

    def weight_term(slot):
        rows = pl.ds(pl.multiple_of(mod(x - slot, nx) * wc, wc), wc)
        return jnp.dot(s["h2t"][rows, :], s["raw2"][...], preferred_element_type=F32)

    u_fill, u_first, u_second, u_last = parts("u", unit_term, ic)
    w_fill, w_first, w_second, w_last = parts("w", weight_term, wc)
    u_fill()
    got_raw.wait_recv()
    w_fill()
    w_first()
    w_second()
    w_last()

    def weight_rows(d):
        return pl.ds(pl.multiple_of(mod(y - d, ny) * wyr, wyr), wyr)

    got_wy = [
        send(s["w_sum"].at[weight_rows(d)], s["wy"].at[d], at(dy=-d)) for d in range(1, ny)
    ]
    u_first()
    value = s["w_own"][weight_rows(0), :]
    for d, copy in enumerate(got_wy, 1):
        copy.wait_recv()
        value = value + s["wy"][d].astype(F32)
    s["wyf"][...] = value

    def weight_block(d):
        return pl.ds(pl.multiple_of(mod(h - d, nh) * wpd, wpd), wpd)

    got_wh = [send(s["wyf"].at[weight_block(d)], s["wh"].at[d], at(dh=-d)) for d in range(1, nh)]
    u_second()
    value = s["wyf"][weight_block(0), :]
    for d, copy in enumerate(got_wh, 1):
        copy.wait_recv()
        value = value + s["wh"][d]
    lc = s["lc"]
    lc[grp] = value
    got_lc = [send(lc.at[grp], lc.at[grp], at(dl=dl, dc=dc)) for dl, dc in others]
    for copy in got_lc:
        copy.wait_recv()
    sides = [functools.reduce(jnp.add, [lc[i * nc + j] for i in range(nl)]) for j in range(nc)]
    weight_sum = jnp.concatenate(sides, axis=1)

    def spread(name, size, value, key):
        buffer = s[name]
        buffer[0] = value
        return [send(buffer.at[0], buffer.at[d], at(**{key: d})) for d in range(1, size)]

    def gather(name, size, copies):
        for copy in copies:
            copy.wait_recv()
        return functools.reduce(jnp.add, [s[name][d] for d in range(size)])

    square = jnp.broadcast_to(jnp.sum(weight_sum * weight_sum, keepdims=True), (8, 128))
    got_sq = spread("sqy", ny, square, "dy")
    u_last()
    got_uy = [
        send(s["u_sum"].at[pl.ds(d * yr, yr)], s["uy"].at[d], at(dy=-d)) for d in range(1, ny)
    ]
    square = gather("sqy", ny, got_sq)
    got_sq = spread("sqh", nh, square, "dh")
    square = gather("sqh", nh, got_sq)
    got_sq = spread("sqx", nx, square, "dx")
    value = s["u_own"][pl.ds(0, yr), :]
    for d, copy in enumerate(got_uy, 1):
        copy.wait_recv()
        value = value + s["uy"][d].astype(F32)
    s["uyf"][...] = value
    got_uh = [
        send(s["uyf"].at[pl.ds(d * ipd, ipd)], s["uh"].at[d], at(dh=-d)) for d in range(1, nh)
    ]
    square = gather("sqx", nx, got_sq)
    mean = square[:1, :1] / (hid * emb)
    wu_ref[...] = weight_sum * lax.rsqrt(mean + EPSILON)
    value = s["uyf"][pl.ds(0, ipd), :]
    for d, copy in enumerate(got_uh, 1):
        copy.wait_recv()
        value = value + s["uh"][d]
    inner = jnp.sum(item_dir * value, axis=-1, keepdims=True)
    ig_ref[...] = item_inv * (value - item_dir * inner)
    for copy in started:
        copy.wait_send()


def ring_scratch(name, rows, cols):
    n = rows // 2
    shapes = {"own": ((rows, cols), F32), "ka": ((n, cols), F32), "kb": ((n, cols), F32)}
    shapes |= {key: ((rows, cols), BF16) for key in ("far", "tr", "tl", "il", "ir", "sum")}
    shapes |= {key: ((n, cols), BF16) for key in ("ia", "ib")}
    return {name + "_" + key: pltpu.VMEM(*shape) for key, shape in shapes.items()}


def step(sizes, query_hidden, query_proj, item_embed, positive, hard_ids):
    nx, ny, nh, nl, nc = sizes
    q, hid = query_hidden.shape
    emb, ipd = query_proj.shape[1], item_embed.shape[0]
    half, wpd = emb // 2, hid // (nx * ny * nh)
    yr, ic = nh * ipd, ny * nh * ipd
    wyr, wc = nh * wpd, ny * nh * wpd
    copies = 128
    scratch = {
        "proj": pltpu.VMEM((hid, emb), BF16),
        "h2": pltpu.VMEM((2 * q, hid), BF16),
        "h2t": pltpu.VMEM((hid, 2 * q), BF16),
        "hbuf": pltpu.VMEM((nh, 2 * ipd, half), BF16),
        "hrow": pltpu.VMEM((yr, emb), F32),
        "g": pltpu.VMEM((nx, ic, emb), BF16),
        "qd": pltpu.VMEM((q, emb), F32),
        "qu": pltpu.VMEM((q, emb), BF16),
        "qinv": pltpu.VMEM((q, 128), F32),
        "e": pltpu.VMEM((nx, q, ic), F32),
        "sg": pltpu.VMEM((nx, q, ic), BF16),
        "raw": pltpu.VMEM((2, q, half), BF16),
        "raw2": pltpu.VMEM((2 * q, half), BF16),
        "wy": pltpu.VMEM((ny, wyr, half), BF16),
        "wyf": pltpu.VMEM((wyr, half), F32),
        "wh": pltpu.VMEM((nh, wpd, half), F32),
        "lc": pltpu.VMEM((nl * nc, wpd, half), F32),
        "uy": pltpu.VMEM((ny, yr, emb), BF16),
        "uyf": pltpu.VMEM((yr, emb), F32),
        "uh": pltpu.VMEM((nh, ipd, emb), F32),
        "sqy": pltpu.VMEM((ny, 8, 128), F32),
        "sqh": pltpu.VMEM((nh, 8, 128), F32),
        "sqx": pltpu.VMEM((nx, 8, 128), F32),
        "send": pltpu.SemaphoreType.DMA((copies,)),
        "recv": pltpu.SemaphoreType.DMA((copies,)),
        "local": pltpu.SemaphoreType.DMA((2,)),
    }
    scratch |= ring_scratch("u", ic, emb)
    scratch |= ring_scratch("w", wc, half)
    names = list(scratch)

    def body(*refs):
        kernel(sizes, *refs[:7], dict(zip(names, refs[7:])))

    vmem = pl.BlockSpec(memory_space=pltpu.VMEM)
    anywhere = pl.BlockSpec(memory_space=pl.ANY)
    return pl.pallas_call(
        body,
        out_shape=(
            jax.ShapeDtypeStruct((ipd, emb), F32),
            jax.ShapeDtypeStruct((wpd, emb), F32),
        ),
        in_specs=[anywhere, anywhere, vmem, vmem, vmem],
        out_specs=(vmem, vmem),
        scratch_shapes=list(scratch.values()),
        compiler_params=pltpu.CompilerParams(
            collective_id=0, has_side_effects=True, vmem_limit_bytes=48 * 2**20
        ),
    )(query_hidden, query_proj, item_embed, positive.reshape(1, q), hard_ids.T)


def solution(mesh):
    return jax.shard_map(
        functools.partial(step, (NX, NY, NH, NL, NC)),
        mesh=mesh,
        in_specs=(
            P(("grp", "blk"), None),
            P(),
            P(("grp", "blk"), None),
            P(("grp", "blk")),
            P(("grp", "blk"), None),
        ),
        out_specs=(P(("grp", "blk"), None), P("blk", None)),
        check_vma=False,
    )
```

```python
import functools

import jax
import jax.numpy as jnp
from jax import lax
from jax.experimental import pallas as pl
from jax.experimental.pallas import tpu as pltpu
from jax.sharding import PartitionSpec as P

MESH = pl.DeviceIdType.MESH
F32, BF16 = jnp.float32, jnp.bfloat16
INV_TAU = 50.0
EPSILON = 1e-06

NX, NY, NH, NL, NC = 4, 8, 4, 3, 2


def mod(value, size):
    return lax.rem(value + size, size)


def kernel(sizes, hid_hbm, proj_hbm, item_hbm, pos_hbm, hard_hbm, ig_ref, wu_ref, s):
    nx, ny, nh, nl, nc = sizes
    q, hid = hid_hbm.shape
    emb = proj_hbm.shape[1]
    ipd = item_hbm.shape[0]
    half = emb // 2
    wpd = wu_ref.shape[0]
    yr, ic = nh * ipd, ny * nh * ipd
    wyr, wc = nh * wpd, ny * nh * wpd

    grp, blk = lax.axis_index("grp"), lax.axis_index("blk")
    x, y, h = blk // (ny * nh), (blk // nh) % ny, blk % nh
    l, c = grp // nc, grp % nc

    def at(dx=0, dy=0, dh=0, dl=0, dc=0):
        place = (mod(x + dx, nx) * ny + mod(y + dy, ny)) * nh + mod(h + dh, nh)
        return (mod(l + dl, nl) * nc + mod(c + dc, nc), place)

    started = []

    def send(src, dst, device):
        i = len(started)
        copy = pltpu.make_async_remote_copy(
            src_ref=src,
            dst_ref=dst,
            send_sem=s["send"].at[i],
            recv_sem=s["recv"].at[i],
            device_id=device,
            device_id_type=MESH,
        )
        copy.start()
        started.append(copy)
        return copy

    across = [(dx, dh) for dx in range(nx) for dh in range(nh) if (dx, dh) != (0, 0)]
    along = [(dh, dl) for dh in range(nh) for dl in range(nl) if (dh, dl) != (0, 0)]
    partners = [at(dx=dx, dh=dh) for dx, dh in across]
    partners += [at(dy=d) for d in range(1, ny)]
    partners += [at(dh=dh, dl=dl) for dh, dl in along if dl]
    partners += [at(dx=d, dc=1) for d in range(nx)]
    left, right, far, twin = at(dx=-1), at(dx=1), at(dx=2), at(dc=1)

    barrier = pltpu.get_barrier_semaphore()
    for device in partners:
        pl.semaphore_signal(barrier, inc=1, device_id=device, device_id_type=MESH)

    def load(src, dst, i):
        copy = pltpu.make_async_copy(src, dst, s["local"].at[i])
        copy.start()
        return copy

    def hid_columns(d):
        return hid_hbm.at[:, pl.ds(pl.multiple_of(mod(x + d, nx) * wc, wc), wc)]

    load_item = load(item_hbm, s["item"], 0)
    load_hid = load(hid_hbm, s["hq"], 1)
    load_proj = load(proj_hbm, s["proj"], 2)
    load_own = load(hid_columns(0), s["hx"].at[0, pl.ds(0, q)], 3)
    load_pos = load(pos_hbm, s["pos"], 4)
    load_hard = load(hard_hbm, s["hard"], 5)

    load_item.wait()
    item = s["item"][...].astype(F32)
    item_inv = lax.rsqrt(jnp.sum(item * item, axis=-1, keepdims=True) + EPSILON)
    item_dir = item * item_inv
    s["hbuf"][0] = jnp.concatenate([item_dir[:, :half], item_dir[:, half:]], axis=0).astype(BF16)

    pl.semaphore_wait(barrier, len(partners))
    got_h = [send(s["hbuf"].at[0], s["hbuf"].at[d], at(dh=d)) for d in range(1, nh)]
    got_hx = [
        send(hid_columns(d), s["hx"].at[d, pl.ds(0, q)], at(dx=d)) for d in range(1, nx)
    ]

    load_hid.wait()
    load_proj.wait()
    raw = jnp.dot(s["hq"][...], s["proj"][...], preferred_element_type=F32)
    query_inv = lax.rsqrt(jnp.sum(raw * raw, axis=-1, keepdims=True) + EPSILON)
    s["qd"][...] = raw * query_inv
    qx = s["qx"]
    qx[pl.ds(0, q), :] = s["qd"][...].astype(BF16)
    s["qinv"][...] = jnp.broadcast_to(query_inv, s["qinv"].shape)

    for copy in got_h:
        copy.wait_recv()
    for d in range(nh):
        block = s["hbuf"][d].astype(F32)
        s["hrow"][pl.ds(d * ipd, ipd), :] = jnp.concatenate([block[:ipd], block[ipd:]], axis=1)
    g = s["g"]
    g[0, pl.ds(0, yr), :] = s["hrow"][...].astype(BF16)

    def piece(slot, d):
        return g.at[slot, pl.ds(d * yr, yr)]

    got_y = {d: send(piece(0, 0), piece(0, d), at(dy=d)) for d in range(1, ny)}
    from_left, from_right, from_far = {}, {}, {}

    order = sorted(range(ny), key=lambda d: (min(d, ny - d), d))
    relayed = max(ny - 3, 1)

    def pass_on(i):
        d = order[i]
        from_left[d].wait_recv()
        if i < relayed and i % 2 == 0:
            from_far[d] = send(piece(1, d), piece(2, d), right)
        from_right[d].wait_recv()
        if i < relayed and i % 2 == 1:
            from_far[d] = send(piece(3, d), piece(2, d), left)

    for i, d in enumerate(order):
        if d:
            got_y[d].wait_recv()
        from_left[d] = send(piece(0, d), piece(1, d), right)
        from_right[d] = send(piece(0, d), piece(3, d), left)
        if i >= relayed:
            from_far[d] = send(piece(0, d), piece(2, d), far)
        if i == min(2, ny - 1):
            for copy in got_hx:
                copy.wait_recv()
            load_own.wait()
            got_hid = send(s["hx"].at[:, pl.ds(0, q)], s["hx"].at[:, pl.ds(q, q)], twin)
        if i >= 2:
            pass_on(i - 2)
    got_qx = [send(qx.at[pl.ds(0, q)], qx.at[pl.ds(d * q, q)], at(dx=d)) for d in range(1, nx)]

    def column(ids):
        i, p = ids % ipd, ids // ipd
        hh, p = p % nh, p // nh
        yy, xx = p % ny, p // ny
        return ((mod(x - xx, nx) * ny + mod(y - yy, ny)) * nh + mod(h - hh, nh)) * ipd + i

    load_pos.wait()
    load_hard.wait()
    pos_ref, hard_ref = s["pos"], s["hard"]
    pos = column(jnp.broadcast_to(pos_ref[...], (q, q)).T[:, :1])
    ids = [pos] + [
        column(jnp.broadcast_to(hard_ref[k : k + 1, :], (q, q)).T[:, :1])
        for k in range(hard_ref.shape[0])
    ]
    lane = lax.broadcasted_iota(jnp.int32, (q, ic), 1)
    total = jnp.zeros((q, 1), F32)
    picks = [jnp.zeros((q, 1), F32) for _ in ids]
    for slot in (0, 1, 3, 2):
        if slot == 1:
            for i in range(max(ny - 2, 0), ny):
                pass_on(i)
        if slot == 2:
            for d in range(ny):
                from_far[d].wait_recv()
        scores = lax.dot_general(
            qx[pl.ds(0, q), :], g[slot], (((1,), (1,)), ((), ())), preferred_element_type=F32
        )
        e = jnp.exp(scores * INV_TAU)
        s["e"][slot] = e
        total = total + jnp.sum(e, axis=1, keepdims=True)
        for k, column_of in enumerate(ids):
            hit = lane == column_of - slot * ic
            picks[k] = picks[k] + jnp.sum(jnp.where(hit, e, 0.0), axis=1, keepdims=True)

    weights = [pick / (pick + picks[0]) for pick in picks[1:]]
    extra = 1.0 + functools.reduce(jnp.add, weights)
    inverse = 1.0 / total
    query_grad = jnp.zeros((q, emb), F32)
    for slot in range(nx):
        grad = s["e"][slot] * inverse
        for k, column_of in enumerate(ids):
            hit = lane == column_of - slot * ic
            grad = grad + jnp.where(hit, -extra if k == 0 else weights[k - 1], 0.0)
        s["sg"][slot] = (grad * INV_TAU).astype(BF16)
        query_grad = query_grad + jnp.dot(s["sg"][slot], g[slot], preferred_element_type=F32)

    query_dir = s["qd"][...]
    inner = jnp.sum(query_dir * query_grad, axis=-1, keepdims=True)
    raw_grad = (s["qinv"][:, :1] * (query_grad - query_dir * inner)).astype(BF16)
    s["raw"][0] = raw_grad[:, :half]
    s["raw"][1] = raw_grad[:, half:]
    rx = s["rx"]
    mine, other = s["raw"].at[c], s["raw"].at[mod(c + 1, nc)]
    got_rx = {0: [], 1: [], 2: [], 3: []}
    for d in (1, 3, 2, 0):
        if d:
            got_rx[d].append(send(mine, rx.at[d, pl.ds(0, q)], at(dx=d)))
        got_rx[d].append(send(other, rx.at[d, pl.ds(q, q)], at(dx=d, dc=1)))
    sgx = s["sgx"]
    got_sg = [
        send(s["sg"].at[d], sgx.at[pl.ds((nx - d) * q, q)], at(dx=-d)) for d in range(1, nx)
    ]
    rx[0, pl.ds(0, q), :] = s["raw"][c]
    sgx[pl.ds(0, q), :] = s["sg"][0]
    got_hid.wait_recv()
    for d in range(nx):
        s["hxt"][d] = s["hx"][d].T
    value = jnp.zeros((wc, half), F32)
    for d in (0, 1, 3, 2):
        for copy in got_rx[d]:
            copy.wait_recv()
        value = value + jnp.dot(s["hxt"][d], rx[d], preferred_element_type=F32)
    s["w_own"][...] = value
    s["w_sum"][...] = value.astype(BF16)

    def weight_rows(d):
        return pl.ds(pl.multiple_of(mod(y - d, ny) * wyr, wyr), wyr)

    near = order[1:]
    got_wy = {d: send(s["w_sum"].at[weight_rows(d)], s["wy"].at[d], at(dy=-d)) for d in near}
    for copy in got_sg + got_qx:
        copy.wait_recv()
    value = lax.dot_general(sgx[...], qx[...], (((0,), (0,)), ((), ())), preferred_element_type=F32)
    s["u_own"][...] = value[:yr]
    s["u_sum"][...] = value.astype(BF16)
    value = s["w_own"][weight_rows(0), :]
    for d in near:
        got_wy[d].wait_recv()
        value = value + s["wy"][d].astype(F32)
    s["wyb"][...] = value.astype(BF16)

    def weight_block(d):
        return pl.ds(pl.multiple_of(mod(h - d, nh) * wpd, wpd), wpd)

    wz = s["wz"]
    got_wz = [
        send(s["wyb"].at[weight_block(dh)], wz.at[dh * nl + l], at(dh=-dh, dl=-dl))
        for dh, dl in along
    ]
    got_uy = {
        d: send(s["u_sum"].at[pl.ds(d * yr, yr)], s["uy"].at[d], at(dy=-d)) for d in near
    }
    wz[l] = s["wyb"][weight_block(0), :]
    for copy in got_wz:
        copy.wait_recv()
    value = functools.reduce(jnp.add, [wz[i].astype(F32) for i in range(nh * nl)])
    lc = s["lc"]
    lc[c] = value
    send(lc.at[c], lc.at[c], twin).wait_recv()
    weight_sum = jnp.concatenate([lc[0], lc[1]], axis=1)

    def spread(name, value, devices):
        buffer = s[name]
        buffer[0] = value
        return [send(buffer.at[0], buffer.at[i], device) for i, device in enumerate(devices, 1)]

    def gather(name, copies):
        for copy in copies:
            copy.wait_recv()
        return functools.reduce(jnp.add, [s[name][i] for i in range(len(copies) + 1)])

    square = jnp.broadcast_to(jnp.sum(weight_sum * weight_sum, keepdims=True), (8, 128))
    got_sq = spread("sqy", square, [at(dy=d) for d in range(1, ny)])
    value = s["u_own"][...]
    for d in near:
        got_uy[d].wait_recv()
        value = value + s["uy"][d].astype(F32)
    s["uyf"][...] = value
    square = gather("sqy", got_sq)
    got_sq = spread("sqxh", square, [at(dx=dx, dh=dh) for dx, dh in across])
    got_uh = [
        send(s["uyf"].at[pl.ds(d * ipd, ipd)], s["uh"].at[d], at(dh=-d)) for d in range(1, nh)
    ]
    square = gather("sqxh", got_sq)
    mean = square[:1, :1] / (hid * emb)
    wu_ref[...] = weight_sum * lax.rsqrt(mean + EPSILON)
    value = s["uyf"][pl.ds(0, ipd), :]
    for d, copy in enumerate(got_uh, 1):
        copy.wait_recv()
        value = value + s["uh"][d]
    inner = jnp.sum(item_dir * value, axis=-1, keepdims=True)
    ig_ref[...] = item_inv * (value - item_dir * inner)
    for copy in started:
        copy.wait_send()


def step(sizes, query_hidden, query_proj, item_embed, positive, hard_ids):
    nx, ny, nh, nl, nc = sizes
    q, hid = query_hidden.shape
    emb, ipd = query_proj.shape[1], item_embed.shape[0]
    half, wpd = emb // 2, hid // (nx * ny * nh)
    yr, ic = nh * ipd, ny * nh * ipd
    wyr, wc = nh * wpd, ny * nh * wpd
    copies = 128
    scratch = {
        "proj": pltpu.VMEM((hid, emb), BF16),
        "item": pltpu.VMEM((ipd, emb), BF16),
        "pos": pltpu.VMEM((1, q), jnp.int32),
        "hard": pltpu.VMEM((hard_ids.shape[1], q), jnp.int32),
        "hq": pltpu.VMEM((q, hid), BF16),
        "hx": pltpu.VMEM((nx, nc * q, wc), BF16),
        "hxt": pltpu.VMEM((nx, wc, nc * q), BF16),
        "hbuf": pltpu.VMEM((nh, 2 * ipd, half), BF16),
        "hrow": pltpu.VMEM((yr, emb), F32),
        "g": pltpu.VMEM((nx, ic, emb), BF16),
        "qd": pltpu.VMEM((q, emb), F32),
        "qx": pltpu.VMEM((nx * q, emb), BF16),
        "qinv": pltpu.VMEM((q, 128), F32),
        "e": pltpu.VMEM((nx, q, ic), F32),
        "sg": pltpu.VMEM((nx, q, ic), BF16),
        "sgx": pltpu.VMEM((nx * q, ic), BF16),
        "raw": pltpu.VMEM((nc, q, half), BF16),
        "rx": pltpu.VMEM((nx, nc * q, half), BF16),
        "w_own": pltpu.VMEM((wc, half), F32),
        "w_sum": pltpu.VMEM((wc, half), BF16),
        "wy": pltpu.VMEM((ny, wyr, half), BF16),
        "wyb": pltpu.VMEM((wyr, half), BF16),
        "wz": pltpu.VMEM((nh * nl, wpd, half), BF16),
        "lc": pltpu.VMEM((nc, wpd, half), F32),
        "u_own": pltpu.VMEM((yr, emb), F32),
        "u_sum": pltpu.VMEM((ic, emb), BF16),
        "uy": pltpu.VMEM((ny, yr, emb), BF16),
        "uyf": pltpu.VMEM((yr, emb), F32),
        "uh": pltpu.VMEM((nh, ipd, emb), F32),
        "sqy": pltpu.VMEM((ny, 8, 128), F32),
        "sqxh": pltpu.VMEM((nx * nh, 8, 128), F32),
        "send": pltpu.SemaphoreType.DMA((copies,)),
        "recv": pltpu.SemaphoreType.DMA((copies,)),
        "local": pltpu.SemaphoreType.DMA((6,)),
    }
    names = list(scratch)

    def body(*refs):
        kernel(sizes, *refs[:7], dict(zip(names, refs[7:])))

    vmem = pl.BlockSpec(memory_space=pltpu.VMEM)
    anywhere = pl.BlockSpec(memory_space=pltpu.HBM)
    return pl.pallas_call(
        body,
        out_shape=(
            jax.ShapeDtypeStruct((ipd, emb), F32),
            jax.ShapeDtypeStruct((wpd, emb), F32),
        ),
        in_specs=[anywhere] * 5,
        out_specs=(vmem, vmem),
        scratch_shapes=list(scratch.values()),
        compiler_params=pltpu.CompilerParams(
            collective_id=0, has_side_effects=True, vmem_limit_bytes=63 * 2**20
        ),
    )(query_hidden, query_proj, item_embed, positive.reshape(1, q), hard_ids.T)


def solution(mesh):
    return jax.shard_map(
        functools.partial(step, (NX, NY, NH, NL, NC)),
        mesh=mesh,
        in_specs=(
            P(("grp", "blk"), None),
            P(),
            P(("grp", "blk"), None),
            P(("grp", "blk")),
            P(("grp", "blk"), None),
        ),
        out_specs=(P(("grp", "blk"), None), P("blk", None)),
        check_vma=False,
    )
```

```python
import functools

import jax
import jax.numpy as jnp
from jax import lax
from jax.experimental import pallas as pl
from jax.experimental.pallas import tpu as pltpu
from jax.sharding import PartitionSpec as P

MESH = pl.DeviceIdType.MESH
F32, BF16 = jnp.float32, jnp.bfloat16
INV_TAU = 50.0
EPSILON = 1e-06

NX, NY, NH, NL, NC = 4, 8, 4, 3, 2


def mod(value, size):
    return lax.rem(value + size, size)


def kernel(sizes, hid_hbm, proj_hbm, item_hbm, pos_hbm, hard_hbm, ig_ref, wu_ref, s):
    nx, ny, nh, nl, nc = sizes
    q, hid = hid_hbm.shape
    emb = proj_hbm.shape[1]
    ipd = item_hbm.shape[0]
    half = emb // 2
    wpd = wu_ref.shape[0]
    yr, ic = nh * ipd, ny * nh * ipd
    wyr, wc = nh * wpd, ny * nh * wpd

    grp, blk = lax.axis_index("grp"), lax.axis_index("blk")
    x, y, h = blk // (ny * nh), (blk // nh) % ny, blk % nh
    l, c = grp // nc, grp % nc

    def at(dx=0, dy=0, dh=0, dl=0, dc=0):
        place = (mod(x + dx, nx) * ny + mod(y + dy, ny)) * nh + mod(h + dh, nh)
        return (mod(l + dl, nl) * nc + mod(c + dc, nc), place)

    started = []

    def send(src, dst, device):
        i = len(started)
        copy = pltpu.make_async_remote_copy(
            src_ref=src,
            dst_ref=dst,
            send_sem=s["send"].at[i],
            recv_sem=s["recv"].at[i],
            device_id=device,
            device_id_type=MESH,
        )
        copy.start()
        started.append(copy)
        return copy

    across = [(dx, dh) for dx in range(nx) for dh in range(nh) if (dx, dh) != (0, 0)]
    along = [(dh, dl) for dh in range(nh) for dl in range(nl) if (dh, dl) != (0, 0)]
    partners = [at(dx=d) for d in range(1, nx)]
    partners += [at(dy=d) for d in range(1, ny)]
    partners += [at(dh=d) for d in range(1, nh)]
    partners += [at(dl=d) for d in range(1, nl)]
    partners += [at(dc=1)]
    left, right, far, twin = at(dx=-1), at(dx=1), at(dx=2), at(dc=1)

    barrier = pltpu.get_barrier_semaphore()
    for device in partners:
        pl.semaphore_signal(barrier, inc=1, device_id=device, device_id_type=MESH)

    def load(src, dst, i):
        copy = pltpu.make_async_copy(src, dst, s["local"].at[i])
        copy.start()
        return copy

    def hid_columns(d):
        return hid_hbm.at[:, pl.ds(pl.multiple_of(mod(x + d, nx) * wc, wc), wc)]

    load_item = load(item_hbm, s["item"], 0)
    load_hid = load(hid_hbm, s["hq"], 1)
    load_proj = load(proj_hbm, s["proj"], 2)
    load_own = load(hid_columns(0), s["hx"].at[0, pl.ds(0, q)], 3)
    load_pos = load(pos_hbm, s["pos"], 4)
    load_hard = load(hard_hbm, s["hard"], 5)

    load_item.wait()
    item = s["item"][...].astype(F32)
    item_inv = lax.rsqrt(jnp.sum(item * item, axis=-1, keepdims=True) + EPSILON)
    item_dir = item * item_inv
    s["hbuf"][0] = jnp.concatenate([item_dir[:, :half], item_dir[:, half:]], axis=0).astype(BF16)

    pl.semaphore_wait(barrier, len(partners))
    got_h = [send(s["hbuf"].at[0], s["hbuf"].at[d], at(dh=d)) for d in range(1, nh)]
    got_hx = [
        send(hid_columns(d), s["hx"].at[d, pl.ds(0, q)], at(dx=d)) for d in range(1, nx)
    ]

    load_hid.wait()
    load_proj.wait()
    raw = jnp.dot(s["hq"][...], s["proj"][...], preferred_element_type=F32)
    query_inv = lax.rsqrt(jnp.sum(raw * raw, axis=-1, keepdims=True) + EPSILON)
    s["qd"][...] = raw * query_inv
    qx = s["qx"]
    qx[pl.ds(0, q), :] = s["qd"][...].astype(BF16)
    s["qinv"][...] = jnp.broadcast_to(query_inv, s["qinv"].shape)

    for copy in got_h:
        copy.wait_recv()
    for d in range(nh):
        block = s["hbuf"][d].astype(F32)
        s["hrow"][pl.ds(d * ipd, ipd), :] = jnp.concatenate([block[:ipd], block[ipd:]], axis=1)
    g = s["g"]
    g[0, pl.ds(0, yr), :] = s["hrow"][...].astype(BF16)

    def piece(slot, d):
        return g.at[slot, pl.ds(d * yr, yr)]

    got_y = {d: send(piece(0, 0), piece(0, d), at(dy=d)) for d in range(1, ny)}
    from_left, from_right, from_far = {}, {}, {}

    order = sorted(range(ny), key=lambda d: (min(d, ny - d), d))
    relayed, lag = max(ny // 2, 1), 4

    def pass_on(i):
        d = order[i]
        from_left[d].wait_recv()
        if i < relayed and i % 2 == 0:
            from_far[d] = send(piece(1, d), piece(2, d), right)
        from_right[d].wait_recv()
        if i < relayed and i % 2 == 1:
            from_far[d] = send(piece(3, d), piece(2, d), left)

    for i, d in enumerate(order):
        if d:
            got_y[d].wait_recv()
        from_left[d] = send(piece(0, d), piece(1, d), right)
        from_right[d] = send(piece(0, d), piece(3, d), left)
        if i >= relayed:
            from_far[d] = send(piece(0, d), piece(2, d), far)
        if i == min(2, ny - 1):
            for copy in got_hx:
                copy.wait_recv()
            load_own.wait()
            got_hid = send(s["hx"].at[:, pl.ds(0, q)], s["hx"].at[:, pl.ds(q, q)], twin)
        if i >= lag:
            pass_on(i - lag)

    def column(ids):
        i, p = ids % ipd, ids // ipd
        hh, p = p % nh, p // nh
        yy, xx = p % ny, p // ny
        return ((mod(x - xx, nx) * ny + mod(y - yy, ny)) * nh + mod(h - hh, nh)) * ipd + i

    load_pos.wait()
    load_hard.wait()
    pos_ref, hard_ref = s["pos"], s["hard"]
    pos = column(jnp.broadcast_to(pos_ref[...], (q, q)).T[:, :1])
    ids = [pos] + [
        column(jnp.broadcast_to(hard_ref[k : k + 1, :], (q, q)).T[:, :1])
        for k in range(hard_ref.shape[0])
    ]
    lane = lax.broadcasted_iota(jnp.int32, (q, ic), 1)
    total = jnp.zeros((q, 1), F32)
    picks = [jnp.zeros((q, 1), F32) for _ in ids]
    for slot in (0, 1, 3, 2):
        if slot == 1:
            for i in range(max(ny - lag, 0), ny):
                pass_on(i)
        if slot == 2:
            for d in range(ny):
                from_far[d].wait_recv()
        scores = lax.dot_general(
            qx[pl.ds(0, q), :], g[slot], (((1,), (1,)), ((), ())), preferred_element_type=F32
        )
        e = jnp.exp(scores * INV_TAU)
        s["e"][slot] = e
        total = total + jnp.sum(e, axis=1, keepdims=True)
        for k, column_of in enumerate(ids):
            hit = lane == column_of - slot * ic
            picks[k] = picks[k] + jnp.sum(jnp.where(hit, e, 0.0), axis=1, keepdims=True)

    weights = [pick / (pick + picks[0]) for pick in picks[1:]]
    extra = 1.0 + functools.reduce(jnp.add, weights)
    inverse = 1.0 / total
    query_grad = jnp.zeros((q, emb), F32)
    for slot in range(nx):
        grad = s["e"][slot] * inverse
        for k, column_of in enumerate(ids):
            hit = lane == column_of - slot * ic
            grad = grad + jnp.where(hit, -extra if k == 0 else weights[k - 1], 0.0)
        s["sg"][slot] = (grad * INV_TAU).astype(BF16)
        query_grad = query_grad + jnp.dot(s["sg"][slot], g[slot], preferred_element_type=F32)

    query_dir = s["qd"][...]
    inner = jnp.sum(query_dir * query_grad, axis=-1, keepdims=True)
    raw_grad = (s["qinv"][:, :1] * (query_grad - query_dir * inner)).astype(BF16)
    s["raw"][0] = raw_grad[:, :half]
    s["raw"][1] = raw_grad[:, half:]
    rx = s["rx"]
    got_hid.wait_recv()
    mine, other = s["raw"].at[c], s["raw"].at[mod(c + 1, nc)]
    got_rx = {0: [], 1: [], 2: [], 3: []}
    for d in (1, 3, 2, 0):
        if d:
            got_rx[d].append(send(mine, rx.at[d, pl.ds(0, q)], at(dx=d)))
        got_rx[d].append(send(other, rx.at[d, pl.ds(q, q)], at(dx=d, dc=1)))
    rx[0, pl.ds(0, q), :] = s["raw"][c]
    for d in range(nx):
        s["hxt"][d] = s["hx"][d].T
    value = jnp.zeros((wc, half), F32)
    for d in (0, 1, 3, 2):
        for copy in got_rx[d]:
            copy.wait_recv()
        value = value + jnp.dot(s["hxt"][d], rx[d], preferred_element_type=F32)
    s["w_own"][...] = value
    s["w_sum"][...] = value.astype(BF16)

    def weight_rows(d):
        return pl.ds(pl.multiple_of(mod(y - d, ny) * wyr, wyr), wyr)

    near = order[1:]
    got_wy = {d: send(s["w_sum"].at[weight_rows(d)], s["wy"].at[d], at(dy=-d)) for d in near}
    sgx = s["sgx"]
    got_sg = [send(qx.at[pl.ds(0, q)], qx.at[pl.ds(d * q, q)], at(dx=d)) for d in range(1, nx)]
    got_sg += [
        send(s["sg"].at[d], sgx.at[pl.ds((nx - d) * q, q)], at(dx=-d)) for d in range(1, nx)
    ]
    sgx[pl.ds(0, q), :] = s["sg"][0]
    value = s["w_own"][weight_rows(0), :]
    for d in near:
        got_wy[d].wait_recv()
        value = value + s["wy"][d].astype(F32)
    s["wyb"][...] = value.astype(BF16)

    def weight_block(d):
        return pl.ds(pl.multiple_of(mod(h - d, nh) * wpd, wpd), wpd)

    wz = s["wz"]
    got_wz = [
        send(s["wyb"].at[weight_block(dh)], wz.at[dh * nl + l], at(dh=-dh, dl=-dl))
        for dh, dl in along
    ]
    for copy in got_sg:
        copy.wait_recv()
    value = lax.dot_general(sgx[...], qx[...], (((0,), (0,)), ((), ())), preferred_element_type=F32)
    s["u_own"][...] = value[:yr]
    s["u_sum"][...] = value.astype(BF16)
    got_uy = {
        d: send(s["u_sum"].at[pl.ds(d * yr, yr)], s["uy"].at[d], at(dy=-d)) for d in near
    }
    wz[l] = s["wyb"][weight_block(0), :]
    for copy in got_wz:
        copy.wait_recv()
    value = functools.reduce(jnp.add, [wz[i].astype(F32) for i in range(nh * nl)])
    lc = s["lc"]
    lc[c] = value
    send(lc.at[c], lc.at[c], twin).wait_recv()
    weight_sum = jnp.concatenate([lc[0], lc[1]], axis=1)

    def spread(name, value, devices):
        buffer = s[name]
        buffer[0] = value
        return [send(buffer.at[0], buffer.at[i], device) for i, device in enumerate(devices, 1)]

    def gather(name, copies):
        for copy in copies:
            copy.wait_recv()
        return functools.reduce(jnp.add, [s[name][i] for i in range(len(copies) + 1)])

    square = jnp.broadcast_to(jnp.sum(weight_sum * weight_sum, keepdims=True), (8, 128))
    got_sq = spread("sqy", square, [at(dy=d) for d in range(1, ny)])
    value = s["u_own"][...]
    for d in near:
        got_uy[d].wait_recv()
        value = value + s["uy"][d].astype(F32)
    s["uyf"][...] = value
    square = gather("sqy", got_sq)
    got_sq = spread("sqxh", square, [at(dx=dx, dh=dh) for dx, dh in across])
    got_uh = [
        send(s["uyf"].at[pl.ds(d * ipd, ipd)], s["uh"].at[d], at(dh=-d)) for d in range(1, nh)
    ]
    square = gather("sqxh", got_sq)
    mean = square[:1, :1] / (hid * emb)
    wu_ref[...] = weight_sum * lax.rsqrt(mean + EPSILON)
    value = s["uyf"][pl.ds(0, ipd), :]
    for d, copy in enumerate(got_uh, 1):
        copy.wait_recv()
        value = value + s["uh"][d]
    inner = jnp.sum(item_dir * value, axis=-1, keepdims=True)
    ig_ref[...] = item_inv * (value - item_dir * inner)
    for copy in started:
        copy.wait_send()


def step(sizes, query_hidden, query_proj, item_embed, positive, hard_ids):
    nx, ny, nh, nl, nc = sizes
    q, hid = query_hidden.shape
    emb, ipd = query_proj.shape[1], item_embed.shape[0]
    half, wpd = emb // 2, hid // (nx * ny * nh)
    yr, ic = nh * ipd, ny * nh * ipd
    wyr, wc = nh * wpd, ny * nh * wpd
    copies = 128
    scratch = {
        "proj": pltpu.VMEM((hid, emb), BF16),
        "item": pltpu.VMEM((ipd, emb), BF16),
        "pos": pltpu.VMEM((1, q), jnp.int32),
        "hard": pltpu.VMEM((hard_ids.shape[1], q), jnp.int32),
        "hq": pltpu.VMEM((q, hid), BF16),
        "hx": pltpu.VMEM((nx, nc * q, wc), BF16),
        "hxt": pltpu.VMEM((nx, wc, nc * q), BF16),
        "hbuf": pltpu.VMEM((nh, 2 * ipd, half), BF16),
        "hrow": pltpu.VMEM((yr, emb), F32),
        "g": pltpu.VMEM((nx, ic, emb), BF16),
        "qd": pltpu.VMEM((q, emb), F32),
        "qx": pltpu.VMEM((nx * q, emb), BF16),
        "qinv": pltpu.VMEM((q, 128), F32),
        "e": pltpu.VMEM((nx, q, ic), F32),
        "sg": pltpu.VMEM((nx, q, ic), BF16),
        "sgx": pltpu.VMEM((nx * q, ic), BF16),
        "raw": pltpu.VMEM((nc, q, half), BF16),
        "rx": pltpu.VMEM((nx, nc * q, half), BF16),
        "w_own": pltpu.VMEM((wc, half), F32),
        "w_sum": pltpu.VMEM((wc, half), BF16),
        "wy": pltpu.VMEM((ny, wyr, half), BF16),
        "wyb": pltpu.VMEM((wyr, half), BF16),
        "wz": pltpu.VMEM((nh * nl, wpd, half), BF16),
        "lc": pltpu.VMEM((nc, wpd, half), F32),
        "u_own": pltpu.VMEM((yr, emb), F32),
        "u_sum": pltpu.VMEM((ic, emb), BF16),
        "uy": pltpu.VMEM((ny, yr, emb), BF16),
        "uyf": pltpu.VMEM((yr, emb), F32),
        "uh": pltpu.VMEM((nh, ipd, emb), F32),
        "sqy": pltpu.VMEM((ny, 8, 128), F32),
        "sqxh": pltpu.VMEM((nx * nh, 8, 128), F32),
        "send": pltpu.SemaphoreType.DMA((copies,)),
        "recv": pltpu.SemaphoreType.DMA((copies,)),
        "local": pltpu.SemaphoreType.DMA((6,)),
    }
    names = list(scratch)

    def body(*refs):
        kernel(sizes, *refs[:7], dict(zip(names, refs[7:])))

    vmem = pl.BlockSpec(memory_space=pltpu.VMEM)
    anywhere = pl.BlockSpec(memory_space=pltpu.HBM)
    return pl.pallas_call(
        body,
        out_shape=(
            jax.ShapeDtypeStruct((ipd, emb), F32),
            jax.ShapeDtypeStruct((wpd, emb), F32),
        ),
        in_specs=[anywhere] * 5,
        out_specs=(vmem, vmem),
        scratch_shapes=list(scratch.values()),
        compiler_params=pltpu.CompilerParams(
            collective_id=0, has_side_effects=True, vmem_limit_bytes=63 * 2**20
        ),
    )(query_hidden, query_proj, item_embed, positive.reshape(1, q), hard_ids.T)


def solution(mesh):
    return jax.shard_map(
        functools.partial(step, (NX, NY, NH, NL, NC)),
        mesh=mesh,
        in_specs=(
            P(("grp", "blk"), None),
            P(),
            P(("grp", "blk"), None),
            P(("grp", "blk")),
            P(("grp", "blk"), None),
        ),
        out_specs=(P(("grp", "blk"), None), P("blk", None)),
        check_vma=False,
    )
```

```python
import functools

import jax
import jax.numpy as jnp
from jax import lax
from jax.experimental import pallas as pl
from jax.experimental.pallas import tpu as pltpu
from jax.sharding import PartitionSpec as P

MESH = pl.DeviceIdType.MESH
F32, BF16 = jnp.float32, jnp.bfloat16
INV_TAU = 50.0
EPSILON = 1e-06
SIDE_AT = 3

NX, NY, NH, NL, NC = 4, 8, 4, 3, 2


def mod(value, size):
    return lax.rem(value + size, size)


def kernel(sizes, hid_hbm, proj_hbm, item_hbm, pos_hbm, hard_hbm, ig_ref, wu_ref, s):
    nx, ny, nh, nl, nc = sizes
    q, hid = hid_hbm.shape
    emb = proj_hbm.shape[1]
    ipd = item_hbm.shape[0]
    half = emb // 2
    wpd = wu_ref.shape[0]
    yr, ic = nh * ipd, ny * nh * ipd
    wyr, wc = nh * wpd, ny * nh * wpd

    grp, blk = lax.axis_index("grp"), lax.axis_index("blk")
    x, y, h = blk // (ny * nh), (blk // nh) % ny, blk % nh
    l, c = grp // nc, grp % nc

    def at(dx=0, dy=0, dh=0, dl=0, dc=0):
        place = (mod(x + dx, nx) * ny + mod(y + dy, ny)) * nh + mod(h + dh, nh)
        return (mod(l + dl, nl) * nc + mod(c + dc, nc), place)

    started = []

    def send(src, dst, device):
        i = len(started)
        copy = pltpu.make_async_remote_copy(
            src_ref=src,
            dst_ref=dst,
            send_sem=s["send"].at[i],
            recv_sem=s["recv"].at[i],
            device_id=device,
            device_id_type=MESH,
        )
        copy.start()
        started.append(copy)
        return copy

    across = [(dx, dh) for dx in range(nx) for dh in range(nh) if (dx, dh) != (0, 0)]
    along = [(dh, dl) for dh in range(nh) for dl in range(nl) if (dh, dl) != (0, 0)]
    partners = [at(dx=d) for d in range(1, nx)]
    partners += [at(dy=d) for d in range(1, ny)]
    partners += [at(dh=d) for d in range(1, nh)]
    partners += [at(dl=d) for d in range(1, nl)]
    partners += [at(dc=1)]
    left, right, far, twin = at(dx=-1), at(dx=1), at(dx=2), at(dc=1)

    barrier = pltpu.get_barrier_semaphore()
    for device in partners:
        pl.semaphore_signal(barrier, inc=1, device_id=device, device_id_type=MESH)

    def load(src, dst, i):
        copy = pltpu.make_async_copy(src, dst, s["local"].at[i])
        copy.start()
        return copy

    def hid_columns(d):
        return hid_hbm.at[:, pl.ds(pl.multiple_of(mod(x + d, nx) * wc, wc), wc)]

    load_item = load(item_hbm, s["item"], 0)
    load_hid = load(hid_hbm, s["hq"], 1)
    load_proj = load(proj_hbm, s["proj"], 2)
    load_own = load(hid_columns(0), s["hx"].at[0, pl.ds(0, q)], 3)
    load_pos = load(pos_hbm, s["pos"], 4)
    load_hard = load(hard_hbm, s["hard"], 5)

    load_item.wait()
    item = s["item"][...].astype(F32)
    item_inv = lax.rsqrt(jnp.sum(item * item, axis=-1, keepdims=True) + EPSILON)
    item_dir = item * item_inv
    s["hbuf"][0] = jnp.concatenate([item_dir[:, :half], item_dir[:, half:]], axis=0).astype(BF16)

    pl.semaphore_wait(barrier, len(partners))
    got_h = [send(s["hbuf"].at[0], s["hbuf"].at[d], at(dh=d)) for d in range(1, nh)]
    got_hx = [
        send(hid_columns(d), s["hx"].at[d, pl.ds(0, q)], at(dx=d)) for d in range(1, nx)
    ]

    load_hid.wait()
    load_proj.wait()
    raw = jnp.dot(s["hq"][...], s["proj"][...], preferred_element_type=F32)
    query_inv = lax.rsqrt(jnp.sum(raw * raw, axis=-1, keepdims=True) + EPSILON)
    s["qd"][...] = raw * query_inv
    qx = s["qx"]
    qx[pl.ds(0, q), :] = s["qd"][...].astype(BF16)
    s["qinv"][...] = jnp.broadcast_to(query_inv, s["qinv"].shape)

    for copy in got_h:
        copy.wait_recv()
    for d in range(nh):
        block = s["hbuf"][d].astype(F32)
        s["hrow"][pl.ds(d * ipd, ipd), :] = jnp.concatenate([block[:ipd], block[ipd:]], axis=1)
    g = s["g"]
    g[0, pl.ds(0, yr), :] = s["hrow"][...].astype(BF16)

    def piece(slot, d):
        return g.at[slot, pl.ds(d * yr, yr)]

    got_y = {d: send(piece(0, 0), piece(0, d), at(dy=d)) for d in range(1, ny)}
    order = sorted(range(ny), key=lambda d: (min(d, ny - d), d))
    side = emb // 4
    main, aside = pl.ds(0, emb - side), pl.ds(emb - side, side)
    got_x = {1: [], 3: [], 2: []}
    for i, d in enumerate(order):
        if d:
            got_y[d].wait_recv()
        for slot, device in ((1, right), (3, left), (2, far)):
            if d:
                rows = pl.ds(d * yr, yr)
                copy = send(g.at[0, rows, main], g.at[slot, rows, main], device)
            else:
                copy = send(piece(0, 0), piece(slot, 0), device)
            got_x[slot].append(copy)
        if i == min(SIDE_AT, ny - 1):
            for slot in got_x:
                got_x[slot].pop(0).wait_recv()
            far_slots = pl.ds(1, nx - 1)
            got_side = [
                send(
                    g.at[far_slots, pl.ds(0, yr), aside],
                    g.at[far_slots, pl.ds(k * yr, yr), aside],
                    at(dy=k),
                )
                for k in order[1:]
            ]
        if i == min(2, ny - 1):
            for copy in got_hx:
                copy.wait_recv()
            load_own.wait()
            got_hid = send(s["hx"].at[:, pl.ds(0, q)], s["hx"].at[:, pl.ds(q, q)], twin)

    def column(ids):
        i, p = ids % ipd, ids // ipd
        hh, p = p % nh, p // nh
        yy, xx = p % ny, p // ny
        return ((mod(x - xx, nx) * ny + mod(y - yy, ny)) * nh + mod(h - hh, nh)) * ipd + i

    load_pos.wait()
    load_hard.wait()
    pos_ref, hard_ref = s["pos"], s["hard"]
    pos = column(jnp.broadcast_to(pos_ref[...], (q, q)).T[:, :1])
    ids = [pos] + [
        column(jnp.broadcast_to(hard_ref[k : k + 1, :], (q, q)).T[:, :1])
        for k in range(hard_ref.shape[0])
    ]
    lane = lax.broadcasted_iota(jnp.int32, (q, ic), 1)
    total = jnp.zeros((q, 1), F32)
    picks = [jnp.zeros((q, 1), F32) for _ in ids]
    for slot in (0, 1, 3, 2):
        if slot == 1:
            for copy in got_side:
                copy.wait_recv()
        if slot:
            for copy in got_x[slot]:
                copy.wait_recv()
        scores = lax.dot_general(
            qx[pl.ds(0, q), :], g[slot], (((1,), (1,)), ((), ())), preferred_element_type=F32
        )
        e = jnp.exp(scores * INV_TAU)
        s["e"][slot] = e
        total = total + jnp.sum(e, axis=1, keepdims=True)
        for k, column_of in enumerate(ids):
            hit = lane == column_of - slot * ic
            picks[k] = picks[k] + jnp.sum(jnp.where(hit, e, 0.0), axis=1, keepdims=True)

    weights = [pick / (pick + picks[0]) for pick in picks[1:]]
    extra = 1.0 + functools.reduce(jnp.add, weights)
    inverse = 1.0 / total
    query_grad = jnp.zeros((q, emb), F32)
    for slot in range(nx):
        grad = s["e"][slot] * inverse
        for k, column_of in enumerate(ids):
            hit = lane == column_of - slot * ic
            grad = grad + jnp.where(hit, -extra if k == 0 else weights[k - 1], 0.0)
        s["sg"][slot] = (grad * INV_TAU).astype(BF16)
        query_grad = query_grad + jnp.dot(s["sg"][slot], g[slot], preferred_element_type=F32)

    query_dir = s["qd"][...]
    inner = jnp.sum(query_dir * query_grad, axis=-1, keepdims=True)
    raw_grad = (s["qinv"][:, :1] * (query_grad - query_dir * inner)).astype(BF16)
    s["raw"][0] = raw_grad[:, :half]
    s["raw"][1] = raw_grad[:, half:]
    rx = s["rx"]
    got_hid.wait_recv()
    mine, other = s["raw"].at[c], s["raw"].at[mod(c + 1, nc)]
    got_rx = {0: [], 1: [], 2: [], 3: []}
    for d in (1, 3, 2, 0):
        if d:
            got_rx[d].append(send(mine, rx.at[d, pl.ds(0, q)], at(dx=d)))
        got_rx[d].append(send(other, rx.at[d, pl.ds(q, q)], at(dx=d, dc=1)))
    rx[0, pl.ds(0, q), :] = s["raw"][c]
    for d in range(nx):
        s["hxt"][d] = s["hx"][d].T
    value = jnp.zeros((wc, half), F32)
    for d in (0, 1, 3, 2):
        for copy in got_rx[d]:
            copy.wait_recv()
        value = value + jnp.dot(s["hxt"][d], rx[d], preferred_element_type=F32)
    s["w_own"][...] = value
    s["w_sum"][...] = value.astype(BF16)

    def weight_rows(d):
        return pl.ds(pl.multiple_of(mod(y - d, ny) * wyr, wyr), wyr)

    near = order[1:]
    got_wy = {d: send(s["w_sum"].at[weight_rows(d)], s["wy"].at[d], at(dy=-d)) for d in near}
    sgx = s["sgx"]
    got_sg = [send(qx.at[pl.ds(0, q)], qx.at[pl.ds(d * q, q)], at(dx=d)) for d in range(1, nx)]
    got_sg += [
        send(s["sg"].at[d], sgx.at[pl.ds((nx - d) * q, q)], at(dx=-d)) for d in range(1, nx)
    ]
    sgx[pl.ds(0, q), :] = s["sg"][0]
    value = s["w_own"][weight_rows(0), :]
    for d in near:
        got_wy[d].wait_recv()
        value = value + s["wy"][d].astype(F32)
    s["wyb"][...] = value.astype(BF16)

    def weight_block(d):
        return pl.ds(pl.multiple_of(mod(h - d, nh) * wpd, wpd), wpd)

    wz = s["wz"]
    got_wz = [
        send(s["wyb"].at[weight_block(dh)], wz.at[dh * nl + l], at(dh=-dh, dl=-dl))
        for dh, dl in along
    ]
    for copy in got_sg:
        copy.wait_recv()
    value = lax.dot_general(sgx[...], qx[...], (((0,), (0,)), ((), ())), preferred_element_type=F32)
    s["u_own"][...] = value[:yr]
    s["u_sum"][...] = value.astype(BF16)
    got_uy = {
        d: send(s["u_sum"].at[pl.ds(d * yr, yr)], s["uy"].at[d], at(dy=-d)) for d in near
    }
    wz[l] = s["wyb"][weight_block(0), :]
    for copy in got_wz:
        copy.wait_recv()
    value = functools.reduce(jnp.add, [wz[i].astype(F32) for i in range(nh * nl)])
    lc = s["lc"]
    lc[c] = value
    send(lc.at[c], lc.at[c], twin).wait_recv()
    weight_sum = jnp.concatenate([lc[0], lc[1]], axis=1)

    def spread(name, value, devices):
        buffer = s[name]
        buffer[0] = value
        return [send(buffer.at[0], buffer.at[i], device) for i, device in enumerate(devices, 1)]

    def gather(name, copies):
        for copy in copies:
            copy.wait_recv()
        return functools.reduce(jnp.add, [s[name][i] for i in range(len(copies) + 1)])

    square = jnp.broadcast_to(jnp.sum(weight_sum * weight_sum, keepdims=True), (8, 128))
    got_sq = spread("sqy", square, [at(dy=d) for d in range(1, ny)])
    value = s["u_own"][...]
    for d in near:
        got_uy[d].wait_recv()
        value = value + s["uy"][d].astype(F32)
    s["uyf"][...] = value
    square = gather("sqy", got_sq)
    got_sq = spread("sqxh", square, [at(dx=dx, dh=dh) for dx, dh in across])
    got_uh = [
        send(s["uyf"].at[pl.ds(d * ipd, ipd)], s["uh"].at[d], at(dh=-d)) for d in range(1, nh)
    ]
    square = gather("sqxh", got_sq)
    mean = square[:1, :1] / (hid * emb)
    wu_ref[...] = weight_sum * lax.rsqrt(mean + EPSILON)
    value = s["uyf"][pl.ds(0, ipd), :]
    for d, copy in enumerate(got_uh, 1):
        copy.wait_recv()
        value = value + s["uh"][d]
    inner = jnp.sum(item_dir * value, axis=-1, keepdims=True)
    ig_ref[...] = item_inv * (value - item_dir * inner)
    for copy in started:
        copy.wait_send()


def step(sizes, query_hidden, query_proj, item_embed, positive, hard_ids):
    nx, ny, nh, nl, nc = sizes
    q, hid = query_hidden.shape
    emb, ipd = query_proj.shape[1], item_embed.shape[0]
    half, wpd = emb // 2, hid // (nx * ny * nh)
    yr, ic = nh * ipd, ny * nh * ipd
    wyr, wc = nh * wpd, ny * nh * wpd
    copies = 128
    scratch = {
        "proj": pltpu.VMEM((hid, emb), BF16),
        "item": pltpu.VMEM((ipd, emb), BF16),
        "pos": pltpu.VMEM((1, q), jnp.int32),
        "hard": pltpu.VMEM((hard_ids.shape[1], q), jnp.int32),
        "hq": pltpu.VMEM((q, hid), BF16),
        "hx": pltpu.VMEM((nx, nc * q, wc), BF16),
        "hxt": pltpu.VMEM((nx, wc, nc * q), BF16),
        "hbuf": pltpu.VMEM((nh, 2 * ipd, half), BF16),
        "hrow": pltpu.VMEM((yr, emb), F32),
        "g": pltpu.VMEM((nx, ic, emb), BF16),
        "qd": pltpu.VMEM((q, emb), F32),
        "qx": pltpu.VMEM((nx * q, emb), BF16),
        "qinv": pltpu.VMEM((q, 128), F32),
        "e": pltpu.VMEM((nx, q, ic), F32),
        "sg": pltpu.VMEM((nx, q, ic), BF16),
        "sgx": pltpu.VMEM((nx * q, ic), BF16),
        "raw": pltpu.VMEM((nc, q, half), BF16),
        "rx": pltpu.VMEM((nx, nc * q, half), BF16),
        "w_own": pltpu.VMEM((wc, half), F32),
        "w_sum": pltpu.VMEM((wc, half), BF16),
        "wy": pltpu.VMEM((ny, wyr, half), BF16),
        "wyb": pltpu.VMEM((wyr, half), BF16),
        "wz": pltpu.VMEM((nh * nl, wpd, half), BF16),
        "lc": pltpu.VMEM((nc, wpd, half), F32),
        "u_own": pltpu.VMEM((yr, emb), F32),
        "u_sum": pltpu.VMEM((ic, emb), BF16),
        "uy": pltpu.VMEM((ny, yr, emb), BF16),
        "uyf": pltpu.VMEM((yr, emb), F32),
        "uh": pltpu.VMEM((nh, ipd, emb), F32),
        "sqy": pltpu.VMEM((ny, 8, 128), F32),
        "sqxh": pltpu.VMEM((nx * nh, 8, 128), F32),
        "send": pltpu.SemaphoreType.DMA((copies,)),
        "recv": pltpu.SemaphoreType.DMA((copies,)),
        "local": pltpu.SemaphoreType.DMA((6,)),
    }
    names = list(scratch)

    def body(*refs):
        kernel(sizes, *refs[:7], dict(zip(names, refs[7:])))

    vmem = pl.BlockSpec(memory_space=pltpu.VMEM)
    anywhere = pl.BlockSpec(memory_space=pltpu.HBM)
    return pl.pallas_call(
        body,
        out_shape=(
            jax.ShapeDtypeStruct((ipd, emb), F32),
            jax.ShapeDtypeStruct((wpd, emb), F32),
        ),
        in_specs=[anywhere] * 5,
        out_specs=(vmem, vmem),
        scratch_shapes=list(scratch.values()),
        compiler_params=pltpu.CompilerParams(
            collective_id=0, has_side_effects=True, vmem_limit_bytes=63 * 2**20
        ),
    )(query_hidden, query_proj, item_embed, positive.reshape(1, q), hard_ids.T)


def solution(mesh):
    return jax.shard_map(
        functools.partial(step, (NX, NY, NH, NL, NC)),
        mesh=mesh,
        in_specs=(
            P(("grp", "blk"), None),
            P(),
            P(("grp", "blk"), None),
            P(("grp", "blk")),
            P(("grp", "blk"), None),
        ),
        out_specs=(P(("grp", "blk"), None), P("blk", None)),
        check_vma=False,
    )
```

```python
import functools

import jax
import jax.numpy as jnp
from jax import lax
from jax.experimental import pallas as pl
from jax.experimental.pallas import tpu as pltpu
from jax.sharding import PartitionSpec as P

MESH = pl.DeviceIdType.MESH
F32, BF16 = jnp.float32, jnp.bfloat16
INV_TAU = 50.0
EPSILON = 1e-06
SIDE_AT = 1

NX, NY, NH, NL, NC = 4, 8, 4, 3, 2


def mod(value, size):
    return lax.rem(value + size, size)


def kernel(sizes, hid_hbm, proj_hbm, item_hbm, pos_hbm, hard_hbm, ig_ref, wu_ref, s):
    nx, ny, nh, nl, nc = sizes
    q, hid = hid_hbm.shape
    emb = proj_hbm.shape[1]
    ipd = item_hbm.shape[0]
    half = emb // 2
    wpd = wu_ref.shape[0]
    yr, ic = nh * ipd, ny * nh * ipd
    wyr, wc = nh * wpd, ny * nh * wpd

    grp, blk = lax.axis_index("grp"), lax.axis_index("blk")
    x, y, h = blk // (ny * nh), (blk // nh) % ny, blk % nh
    l, c = grp // nc, grp % nc

    def at(dx=0, dy=0, dh=0, dl=0, dc=0):
        place = (mod(x + dx, nx) * ny + mod(y + dy, ny)) * nh + mod(h + dh, nh)
        return (mod(l + dl, nl) * nc + mod(c + dc, nc), place)

    started = []

    def send(src, dst, device):
        i = len(started)
        copy = pltpu.make_async_remote_copy(
            src_ref=src,
            dst_ref=dst,
            send_sem=s["send"].at[i],
            recv_sem=s["recv"].at[i],
            device_id=device,
            device_id_type=MESH,
        )
        copy.start()
        started.append(copy)
        return copy

    across = [(dx, dh) for dx in range(nx) for dh in range(nh) if (dx, dh) != (0, 0)]
    along = [(dh, dl) for dh in range(nh) for dl in range(nl) if (dh, dl) != (0, 0)]
    partners = [at(dx=d) for d in range(1, nx)]
    partners += [at(dy=d) for d in range(1, ny)]
    partners += [at(dh=d) for d in range(1, nh)]
    partners += [at(dl=d) for d in range(1, nl)]
    partners += [at(dc=1)]
    left, right, far, twin = at(dx=-1), at(dx=1), at(dx=2), at(dc=1)

    barrier = pltpu.get_barrier_semaphore()
    for device in partners:
        pl.semaphore_signal(barrier, inc=1, device_id=device, device_id_type=MESH)

    def load(src, dst, i):
        copy = pltpu.make_async_copy(src, dst, s["local"].at[i])
        copy.start()
        return copy

    def hid_columns(d):
        return hid_hbm.at[:, pl.ds(pl.multiple_of(mod(x + d, nx) * wc, wc), wc)]

    load_item = load(item_hbm, s["item"], 0)
    load_hid = load(hid_hbm, s["hq"], 1)
    load_proj = load(proj_hbm, s["proj"], 2)
    load_own = load(hid_columns(0), s["hx"].at[0, pl.ds(0, q)], 3)
    load_pos = load(pos_hbm, s["pos"], 4)
    load_hard = load(hard_hbm, s["hard"], 5)

    load_item.wait()
    item = s["item"][...].astype(F32)
    item_inv = lax.rsqrt(jnp.sum(item * item, axis=-1, keepdims=True) + EPSILON)
    item_dir = item * item_inv
    s["hbuf"][0] = jnp.concatenate([item_dir[:, :half], item_dir[:, half:]], axis=0).astype(BF16)

    pl.semaphore_wait(barrier, len(partners))
    got_h = [send(s["hbuf"].at[0], s["hbuf"].at[d], at(dh=d)) for d in range(1, nh)]
    got_hx = [
        send(hid_columns(d), s["hx"].at[d, pl.ds(0, q)], at(dx=d)) for d in range(1, nx)
    ]

    load_hid.wait()
    load_proj.wait()
    raw = jnp.dot(s["hq"][...], s["proj"][...], preferred_element_type=F32)
    query_inv = lax.rsqrt(jnp.sum(raw * raw, axis=-1, keepdims=True) + EPSILON)
    s["qd"][...] = raw * query_inv
    qx = s["qx"]
    qx[pl.ds(0, q), :] = s["qd"][...].astype(BF16)
    s["qinv"][...] = jnp.broadcast_to(query_inv, s["qinv"].shape)

    for copy in got_h:
        copy.wait_recv()
    for d in range(nh):
        block = s["hbuf"][d].astype(F32)
        s["hrow"][pl.ds(d * ipd, ipd), :] = jnp.concatenate([block[:ipd], block[ipd:]], axis=1)
    g = s["g"]
    g[0, pl.ds(0, yr), :] = s["hrow"][...].astype(BF16)

    def piece(slot, d):
        return g.at[slot, pl.ds(d * yr, yr)]

    got_y = {d: send(piece(0, 0), piece(0, d), at(dy=d)) for d in range(1, ny)}
    order = sorted(range(ny), key=lambda d: (min(d, ny - d), d))
    side = emb // 4
    main, aside = pl.ds(0, emb - side), pl.ds(emb - side, side)
    got_x = {1: [], 3: [], 2: []}
    for i, d in enumerate(order):
        if d:
            got_y[d].wait_recv()
        for slot, device in ((1, right), (3, left), (2, far)):
            if d:
                rows = pl.ds(d * yr, yr)
                copy = send(g.at[0, rows, main], g.at[slot, rows, main], device)
            else:
                copy = send(piece(0, 0), piece(slot, 0), device)
            got_x[slot].append(copy)
        if i == min(SIDE_AT, ny - 1):
            for slot in got_x:
                got_x[slot].pop(0).wait_recv()
            far_slots = pl.ds(1, nx - 1)
            got_side = [
                send(
                    g.at[far_slots, pl.ds(0, yr), aside],
                    g.at[far_slots, pl.ds(k * yr, yr), aside],
                    at(dy=k),
                )
                for k in order[1:]
            ]
        if i == min(2, ny - 1):
            for copy in got_hx:
                copy.wait_recv()
            load_own.wait()
            got_hid = send(s["hx"].at[:, pl.ds(0, q)], s["hx"].at[:, pl.ds(q, q)], twin)

    def column(ids):
        i, p = ids % ipd, ids // ipd
        hh, p = p % nh, p // nh
        yy, xx = p % ny, p // ny
        return ((mod(x - xx, nx) * ny + mod(y - yy, ny)) * nh + mod(h - hh, nh)) * ipd + i

    load_pos.wait()
    load_hard.wait()
    pos_ref, hard_ref = s["pos"], s["hard"]
    pos = column(jnp.broadcast_to(pos_ref[...], (q, q)).T[:, :1])
    ids = [pos] + [
        column(jnp.broadcast_to(hard_ref[k : k + 1, :], (q, q)).T[:, :1])
        for k in range(hard_ref.shape[0])
    ]
    lane = lax.broadcasted_iota(jnp.int32, (q, ic), 1)
    total = jnp.zeros((q, 1), F32)
    picks = [jnp.zeros((q, 1), F32) for _ in ids]
    for slot in (0, 1, 3, 2):
        if slot == 1:
            for copy in got_side:
                copy.wait_recv()
        if slot:
            for copy in got_x[slot]:
                copy.wait_recv()
        scores = lax.dot_general(
            qx[pl.ds(0, q), :], g[slot], (((1,), (1,)), ((), ())), preferred_element_type=F32
        )
        e = jnp.exp(scores * INV_TAU)
        s["e"][slot] = e
        total = total + jnp.sum(e, axis=1, keepdims=True)
        for k, column_of in enumerate(ids):
            hit = lane == column_of - slot * ic
            picks[k] = picks[k] + jnp.sum(jnp.where(hit, e, 0.0), axis=1, keepdims=True)

    weights = [pick / (pick + picks[0]) for pick in picks[1:]]
    extra = 1.0 + functools.reduce(jnp.add, weights)
    inverse = 1.0 / total
    query_grad = jnp.zeros((q, emb), F32)
    for slot in range(nx):
        grad = s["e"][slot] * inverse
        for k, column_of in enumerate(ids):
            hit = lane == column_of - slot * ic
            grad = grad + jnp.where(hit, -extra if k == 0 else weights[k - 1], 0.0)
        s["sg"][slot] = (grad * INV_TAU).astype(BF16)
        query_grad = query_grad + jnp.dot(s["sg"][slot], g[slot], preferred_element_type=F32)

    query_dir = s["qd"][...]
    inner = jnp.sum(query_dir * query_grad, axis=-1, keepdims=True)
    raw_grad = (s["qinv"][:, :1] * (query_grad - query_dir * inner)).astype(BF16)
    s["raw"][0] = raw_grad[:, :half]
    s["raw"][1] = raw_grad[:, half:]
    rx = s["rx"]
    got_hid.wait_recv()
    mine, other = s["raw"].at[c], s["raw"].at[mod(c + 1, nc)]
    got_rx = {0: [], 1: [], 2: [], 3: []}
    for d in (1, 3, 2, 0):
        if d:
            got_rx[d].append(send(mine, rx.at[d, pl.ds(0, q)], at(dx=d)))
        got_rx[d].append(send(other, rx.at[d, pl.ds(q, q)], at(dx=d, dc=1)))
    rx[0, pl.ds(0, q), :] = s["raw"][c]
    for d in range(nx):
        s["hxt"][d] = s["hx"][d].T
    value = jnp.zeros((wc, half), F32)
    for d in (0, 1, 3, 2):
        for copy in got_rx[d]:
            copy.wait_recv()
        value = value + jnp.dot(s["hxt"][d], rx[d], preferred_element_type=F32)
    s["w_own"][...] = value
    s["w_sum"][...] = value.astype(BF16)

    def weight_rows(d):
        return pl.ds(pl.multiple_of(mod(y - d, ny) * wyr, wyr), wyr)

    near = order[1:]
    got_wy = {d: send(s["w_sum"].at[weight_rows(d)], s["wy"].at[d], at(dy=-d)) for d in near}
    sgx = s["sgx"]
    got_sg = [send(qx.at[pl.ds(0, q)], qx.at[pl.ds(d * q, q)], at(dx=d)) for d in range(1, nx)]
    got_sg += [
        send(s["sg"].at[d], sgx.at[pl.ds((nx - d) * q, q)], at(dx=-d)) for d in range(1, nx)
    ]
    sgx[pl.ds(0, q), :] = s["sg"][0]
    value = s["w_own"][weight_rows(0), :]
    for d in near:
        got_wy[d].wait_recv()
        value = value + s["wy"][d].astype(F32)
    s["wyb"][...] = value.astype(BF16)

    def weight_block(d):
        return pl.ds(pl.multiple_of(mod(h - d, nh) * wpd, wpd), wpd)

    wz = s["wz"]
    got_wz = [
        send(s["wyb"].at[weight_block(dh)], wz.at[dh * nl + l], at(dh=-dh, dl=-dl))
        for dh, dl in along
    ]
    for copy in got_sg:
        copy.wait_recv()
    value = lax.dot_general(sgx[...], qx[...], (((0,), (0,)), ((), ())), preferred_element_type=F32)
    s["u_own"][...] = value[:yr]
    s["u_sum"][...] = value.astype(BF16)
    got_uy = {
        d: send(s["u_sum"].at[pl.ds(d * yr, yr)], s["uy"].at[d], at(dy=-d)) for d in near
    }
    wz[l] = s["wyb"][weight_block(0), :]
    for copy in got_wz:
        copy.wait_recv()
    value = functools.reduce(jnp.add, [wz[i].astype(F32) for i in range(nh * nl)])
    lc = s["lc"]
    lc[c] = value
    send(lc.at[c], lc.at[c], twin).wait_recv()
    weight_sum = jnp.concatenate([lc[0], lc[1]], axis=1)

    def spread(name, value, devices):
        buffer = s[name]
        buffer[0] = value
        return [send(buffer.at[0], buffer.at[i], device) for i, device in enumerate(devices, 1)]

    def gather(name, copies):
        for copy in copies:
            copy.wait_recv()
        return functools.reduce(jnp.add, [s[name][i] for i in range(len(copies) + 1)])

    square = jnp.broadcast_to(jnp.sum(weight_sum * weight_sum, keepdims=True), (8, 128))
    got_sq = spread("sqy", square, [at(dy=d) for d in range(1, ny)])
    value = s["u_own"][...]
    for d in near:
        got_uy[d].wait_recv()
        value = value + s["uy"][d].astype(F32)
    s["uyf"][...] = value
    square = gather("sqy", got_sq)
    got_sq = spread("sqxh", square, [at(dx=dx, dh=dh) for dx, dh in across])
    got_uh = [
        send(s["uyf"].at[pl.ds(d * ipd, ipd)], s["uh"].at[d], at(dh=-d)) for d in range(1, nh)
    ]
    square = gather("sqxh", got_sq)
    mean = square[:1, :1] / (hid * emb)
    wu_ref[...] = weight_sum * lax.rsqrt(mean + EPSILON)
    value = s["uyf"][pl.ds(0, ipd), :]
    for d, copy in enumerate(got_uh, 1):
        copy.wait_recv()
        value = value + s["uh"][d]
    inner = jnp.sum(item_dir * value, axis=-1, keepdims=True)
    ig_ref[...] = item_inv * (value - item_dir * inner)
    for copy in started:
        copy.wait_send()


def step(sizes, query_hidden, query_proj, item_embed, positive, hard_ids):
    nx, ny, nh, nl, nc = sizes
    q, hid = query_hidden.shape
    emb, ipd = query_proj.shape[1], item_embed.shape[0]
    half, wpd = emb // 2, hid // (nx * ny * nh)
    yr, ic = nh * ipd, ny * nh * ipd
    wyr, wc = nh * wpd, ny * nh * wpd
    copies = 128
    scratch = {
        "proj": pltpu.VMEM((hid, emb), BF16),
        "item": pltpu.VMEM((ipd, emb), BF16),
        "pos": pltpu.VMEM((1, q), jnp.int32),
        "hard": pltpu.VMEM((hard_ids.shape[1], q), jnp.int32),
        "hq": pltpu.VMEM((q, hid), BF16),
        "hx": pltpu.VMEM((nx, nc * q, wc), BF16),
        "hxt": pltpu.VMEM((nx, wc, nc * q), BF16),
        "hbuf": pltpu.VMEM((nh, 2 * ipd, half), BF16),
        "hrow": pltpu.VMEM((yr, emb), F32),
        "g": pltpu.VMEM((nx, ic, emb), BF16),
        "qd": pltpu.VMEM((q, emb), F32),
        "qx": pltpu.VMEM((nx * q, emb), BF16),
        "qinv": pltpu.VMEM((q, 128), F32),
        "e": pltpu.VMEM((nx, q, ic), F32),
        "sg": pltpu.VMEM((nx, q, ic), BF16),
        "sgx": pltpu.VMEM((nx * q, ic), BF16),
        "raw": pltpu.VMEM((nc, q, half), BF16),
        "rx": pltpu.VMEM((nx, nc * q, half), BF16),
        "w_own": pltpu.VMEM((wc, half), F32),
        "w_sum": pltpu.VMEM((wc, half), BF16),
        "wy": pltpu.VMEM((ny, wyr, half), BF16),
        "wyb": pltpu.VMEM((wyr, half), BF16),
        "wz": pltpu.VMEM((nh * nl, wpd, half), BF16),
        "lc": pltpu.VMEM((nc, wpd, half), F32),
        "u_own": pltpu.VMEM((yr, emb), F32),
        "u_sum": pltpu.VMEM((ic, emb), BF16),
        "uy": pltpu.VMEM((ny, yr, emb), BF16),
        "uyf": pltpu.VMEM((yr, emb), F32),
        "uh": pltpu.VMEM((nh, ipd, emb), F32),
        "sqy": pltpu.VMEM((ny, 8, 128), F32),
        "sqxh": pltpu.VMEM((nx * nh, 8, 128), F32),
        "send": pltpu.SemaphoreType.DMA((copies,)),
        "recv": pltpu.SemaphoreType.DMA((copies,)),
        "local": pltpu.SemaphoreType.DMA((6,)),
    }
    names = list(scratch)

    def body(*refs):
        kernel(sizes, *refs[:7], dict(zip(names, refs[7:])))

    vmem = pl.BlockSpec(memory_space=pltpu.VMEM)
    anywhere = pl.BlockSpec(memory_space=pltpu.HBM)
    return pl.pallas_call(
        body,
        out_shape=(
            jax.ShapeDtypeStruct((ipd, emb), F32),
            jax.ShapeDtypeStruct((wpd, emb), F32),
        ),
        in_specs=[anywhere] * 5,
        out_specs=(vmem, vmem),
        scratch_shapes=list(scratch.values()),
        compiler_params=pltpu.CompilerParams(
            collective_id=0, has_side_effects=True, vmem_limit_bytes=63 * 2**20
        ),
    )(query_hidden, query_proj, item_embed, positive.reshape(1, q), hard_ids.T)


def solution(mesh):
    return jax.shard_map(
        functools.partial(step, (NX, NY, NH, NL, NC)),
        mesh=mesh,
        in_specs=(
            P(("grp", "blk"), None),
            P(),
            P(("grp", "blk"), None),
            P(("grp", "blk")),
            P(("grp", "blk"), None),
        ),
        out_specs=(P(("grp", "blk"), None), P("blk", None)),
        check_vma=False,
    )
```

```python
import functools

import jax
import jax.numpy as jnp
from jax import lax
from jax.experimental import pallas as pl
from jax.experimental.pallas import tpu as pltpu
from jax.sharding import PartitionSpec as P

MESH = pl.DeviceIdType.MESH
F32, BF16 = jnp.float32, jnp.bfloat16
INV_TAU = 50.0
EPSILON = 1e-06
SIDE_AT = 1

NX, NY, NH, NL, NC = 4, 8, 4, 3, 2


def mod(value, size):
    return lax.rem(value + size, size)


def kernel(sizes, hid_hbm, proj_hbm, item_hbm, pos_hbm, hard_hbm, ig_ref, wu_ref, s):
    nx, ny, nh, nl, nc = sizes
    q, hid = hid_hbm.shape
    emb = proj_hbm.shape[1]
    ipd = item_hbm.shape[0]
    half = emb // 2
    wpd = wu_ref.shape[0]
    yr, ic = nh * ipd, ny * nh * ipd
    wyr, wc = nh * wpd, ny * nh * wpd

    grp, blk = lax.axis_index("grp"), lax.axis_index("blk")
    x, y, h = blk // (ny * nh), (blk // nh) % ny, blk % nh
    l, c = grp // nc, grp % nc

    def at(dx=0, dy=0, dh=0, dl=0, dc=0):
        place = (mod(x + dx, nx) * ny + mod(y + dy, ny)) * nh + mod(h + dh, nh)
        return (mod(l + dl, nl) * nc + mod(c + dc, nc), place)

    started = []

    def send(src, dst, device):
        i = len(started)
        copy = pltpu.make_async_remote_copy(
            src_ref=src,
            dst_ref=dst,
            send_sem=s["send"].at[i],
            recv_sem=s["recv"].at[i],
            device_id=device,
            device_id_type=MESH,
        )
        copy.start()
        started.append(copy)
        return copy

    across = [(dx, dh) for dx in range(nx) for dh in range(nh) if (dx, dh) != (0, 0)]
    along = [(dh, dl) for dh in range(nh) for dl in range(nl) if (dh, dl) != (0, 0)]
    partners = [at(dx=d) for d in range(1, nx)]
    partners += [at(dy=d) for d in range(1, ny)]
    partners += [at(dh=d) for d in range(1, nh)]
    partners += [at(dl=d) for d in range(1, nl)]
    partners += [at(dc=1)]
    left, right, far, twin = at(dx=-1), at(dx=1), at(dx=2), at(dc=1)

    barrier = pltpu.get_barrier_semaphore()
    for device in partners:
        pl.semaphore_signal(barrier, inc=1, device_id=device, device_id_type=MESH)

    def load(src, dst, i):
        copy = pltpu.make_async_copy(src, dst, s["local"].at[i])
        copy.start()
        return copy

    def hid_columns(d):
        return hid_hbm.at[:, pl.ds(pl.multiple_of(mod(x + d, nx) * wc, wc), wc)]

    load_item = load(item_hbm, s["item"], 0)
    load_hid = load(hid_hbm, s["hq"], 1)
    load_proj = load(proj_hbm, s["proj"], 2)
    load_own = load(hid_columns(0), s["hx"].at[0, pl.ds(0, q)], 3)
    load_pos = load(pos_hbm, s["pos"], 4)
    load_hard = load(hard_hbm, s["hard"], 5)

    load_item.wait()
    item = s["item"][...].astype(F32)
    item_inv = lax.rsqrt(jnp.sum(item * item, axis=-1, keepdims=True) + EPSILON)
    item_dir = item * item_inv
    s["hbuf"][0] = jnp.concatenate([item_dir[:, :half], item_dir[:, half:]], axis=0).astype(BF16)

    pl.semaphore_wait(barrier, len(partners))
    got_h = [send(s["hbuf"].at[0], s["hbuf"].at[d], at(dh=d)) for d in range(1, nh)]
    got_hx = [
        send(hid_columns(d), s["hx"].at[d, pl.ds(0, q)], at(dx=d)) for d in range(1, nx)
    ]

    load_hid.wait()
    load_proj.wait()
    raw = jnp.dot(s["hq"][...], s["proj"][...], preferred_element_type=F32)
    query_inv = lax.rsqrt(jnp.sum(raw * raw, axis=-1, keepdims=True) + EPSILON)
    s["qd"][...] = raw * query_inv
    qx = s["qx"]
    qx[pl.ds(0, q), :] = s["qd"][...].astype(BF16)
    s["qinv"][...] = jnp.broadcast_to(query_inv, s["qinv"].shape)

    for copy in got_h:
        copy.wait_recv()
    for d in range(nh):
        block = s["hbuf"][d].astype(F32)
        s["hrow"][pl.ds(d * ipd, ipd), :] = jnp.concatenate([block[:ipd], block[ipd:]], axis=1)
    g = s["g"]
    g[0, pl.ds(0, yr), :] = s["hrow"][...].astype(BF16)

    def piece(slot, d):
        return g.at[slot, pl.ds(d * yr, yr)]

    got_y = {d: send(piece(0, 0), piece(0, d), at(dy=d)) for d in range(1, ny)}
    order = sorted(range(ny), key=lambda d: (min(d, ny - d), d))
    side = emb // 4
    main, aside = pl.ds(0, emb - side), pl.ds(emb - side, side)
    got_x = {1: [], 3: [], 2: []}
    for i, d in enumerate(order):
        if d:
            got_y[d].wait_recv()
        for slot, device in ((1, right), (3, left), (2, far)):
            if d:
                rows = pl.ds(d * yr, yr)
                copy = send(g.at[0, rows, main], g.at[slot, rows, main], device)
            else:
                copy = send(piece(0, 0), piece(slot, 0), device)
            got_x[slot].append(copy)
        if i == min(SIDE_AT, ny - 1):
            for slot in got_x:
                got_x[slot].pop(0).wait_recv()
            far_slots = pl.ds(1, nx - 1)
            got_side = [
                send(
                    g.at[far_slots, pl.ds(0, yr), aside],
                    g.at[far_slots, pl.ds(k * yr, yr), aside],
                    at(dy=k),
                )
                for k in order[1:]
            ]
        if i == min(2, ny - 1):
            for copy in got_hx:
                copy.wait_recv()
            load_own.wait()
            got_hid = send(s["hx"].at[:, pl.ds(0, q)], s["hx"].at[:, pl.ds(q, q)], twin)

    def column(ids):
        i, p = ids % ipd, ids // ipd
        hh, p = p % nh, p // nh
        yy, xx = p % ny, p // ny
        return ((mod(x - xx, nx) * ny + mod(y - yy, ny)) * nh + mod(h - hh, nh)) * ipd + i

    load_pos.wait()
    load_hard.wait()
    pos_ref, hard_ref = s["pos"], s["hard"]
    pos = column(jnp.broadcast_to(pos_ref[...], (q, q)).T[:, :1])
    ids = [pos] + [
        column(jnp.broadcast_to(hard_ref[k : k + 1, :], (q, q)).T[:, :1])
        for k in range(hard_ref.shape[0])
    ]
    lane = lax.broadcasted_iota(jnp.int32, (q, ic), 1)
    total = jnp.zeros((q, 1), F32)
    picks = [jnp.zeros((q, 1), F32) for _ in ids]
    for slot in (0, 1, 3, 2):
        if slot == 1:
            for copy in got_side:
                copy.wait_recv()
        if slot:
            for copy in got_x[slot]:
                copy.wait_recv()
        scores = lax.dot_general(
            qx[pl.ds(0, q), :], g[slot], (((1,), (1,)), ((), ())), preferred_element_type=F32
        )
        e = jnp.exp(scores * INV_TAU)
        s["e"][slot] = e
        total = total + jnp.sum(e, axis=1, keepdims=True)
        for k, column_of in enumerate(ids):
            hit = lane == column_of - slot * ic
            picks[k] = picks[k] + jnp.sum(jnp.where(hit, e, 0.0), axis=1, keepdims=True)

    weights = [pick / (pick + picks[0]) for pick in picks[1:]]
    extra = 1.0 + functools.reduce(jnp.add, weights)
    inverse = 1.0 / total
    query_grad = jnp.zeros((q, emb), F32)
    for slot in range(nx):
        grad = s["e"][slot] * inverse
        for k, column_of in enumerate(ids):
            hit = lane == column_of - slot * ic
            grad = grad + jnp.where(hit, -extra if k == 0 else weights[k - 1], 0.0)
        s["sg"][slot] = (grad * INV_TAU).astype(BF16)
        query_grad = query_grad + jnp.dot(s["sg"][slot], g[slot], preferred_element_type=F32)

    query_dir = s["qd"][...]
    inner = jnp.sum(query_dir * query_grad, axis=-1, keepdims=True)
    raw_grad = (s["qinv"][:, :1] * (query_grad - query_dir * inner)).astype(BF16)
    s["raw"][0] = raw_grad[:, :half]
    s["raw"][1] = raw_grad[:, half:]
    rx = s["rx"]
    got_hid.wait_recv()
    mine, other = s["raw"].at[c], s["raw"].at[mod(c + 1, nc)]
    got_rx = {0: [], 1: [], 2: [], 3: []}
    for d in (1, 3, 2, 0):
        if d:
            got_rx[d].append(send(mine, rx.at[d, pl.ds(0, q)], at(dx=d)))
        got_rx[d].append(send(other, rx.at[d, pl.ds(q, q)], at(dx=d, dc=1)))
    rx[0, pl.ds(0, q), :] = s["raw"][c]
    for d in range(nx):
        s["hxt"][d] = s["hx"][d].T
    value = jnp.zeros((wc, half), F32)
    for d in (0, 1, 3, 2):
        for copy in got_rx[d]:
            copy.wait_recv()
        value = value + jnp.dot(s["hxt"][d], rx[d], preferred_element_type=F32)
    s["w_own"][...] = value
    s["w_sum"][...] = value.astype(BF16)

    def weight_rows(d):
        return pl.ds(pl.multiple_of(mod(y - d, ny) * wyr, wyr), wyr)

    near = order[1:]
    got_wy = {d: send(s["w_sum"].at[weight_rows(d)], s["wy"].at[d], at(dy=-d)) for d in near}
    sgx = s["sgx"]
    got_sg = [send(qx.at[pl.ds(0, q)], qx.at[pl.ds(d * q, q)], at(dx=d)) for d in range(1, nx)]
    got_sg += [
        send(s["sg"].at[d], sgx.at[pl.ds((nx - d) * q, q)], at(dx=-d)) for d in range(1, nx)
    ]
    sgx[pl.ds(0, q), :] = s["sg"][0]
    value = s["w_own"][weight_rows(0), :]
    for d in near:
        got_wy[d].wait_recv()
        value = value + s["wy"][d].astype(F32)
    s["wyb"][...] = value.astype(BF16)

    def weight_block(d):
        return pl.ds(pl.multiple_of(mod(h - d, nh) * wpd, wpd), wpd)

    wz = s["wz"]
    got_wz = [
        send(s["wyb"].at[weight_block(dh)], wz.at[dh * nl + l], at(dh=-dh, dl=-dl))
        for dh, dl in along
    ]
    for copy in got_sg:
        copy.wait_recv()
    value = lax.dot_general(sgx[...], qx[...], (((0,), (0,)), ((), ())), preferred_element_type=F32)
    s["u_own"][...] = value[:yr]
    s["u_sum"][...] = value.astype(BF16)
    got_uy = {
        d: send(s["u_sum"].at[pl.ds(d * yr, yr)], s["uy"].at[d], at(dy=-d)) for d in near
    }
    wz[l] = s["wyb"][weight_block(0), :]
    for copy in got_wz:
        copy.wait_recv()
    value = functools.reduce(jnp.add, [wz[i].astype(F32) for i in range(nh * nl)])
    lc = s["lc"]
    lc[c] = value
    got_lc = send(lc.at[c], lc.at[c], twin)

    def spread(name, value, devices):
        buffer = s[name]
        buffer[0] = value
        return [send(buffer.at[0], buffer.at[i], device) for i, device in enumerate(devices, 1)]

    def gather(name, copies):
        for copy in copies:
            copy.wait_recv()
        return functools.reduce(jnp.add, [s[name][i] for i in range(len(copies) + 1)])

    sqy = s["sqy"]
    sqy[c] = jnp.broadcast_to(jnp.sum(value * value, keepdims=True), (8, 128))
    places = [(dy, dc) for dy in range(ny) for dc in range(nc) if (dy, dc) != (0, 0)]
    got_sq = [send(sqy.at[c], sqy.at[dy * nc + c], at(dy=dy, dc=dc)) for dy, dc in places]
    value = s["u_own"][...]
    for d in near:
        got_uy[d].wait_recv()
        value = value + s["uy"][d].astype(F32)
    s["uyf"][...] = value
    square = gather("sqy", got_sq)
    got_lc.wait_recv()
    weight_sum = jnp.concatenate([lc[0], lc[1]], axis=1)
    got_sq = spread("sqxh", square, [at(dx=dx, dh=dh) for dx, dh in across])
    got_uh = [
        send(s["uyf"].at[pl.ds(d * ipd, ipd)], s["uh"].at[d], at(dh=-d)) for d in range(1, nh)
    ]
    square = gather("sqxh", got_sq)
    mean = square[:1, :1] / (hid * emb)
    wu_ref[...] = weight_sum * lax.rsqrt(mean + EPSILON)
    value = s["uyf"][pl.ds(0, ipd), :]
    for d, copy in enumerate(got_uh, 1):
        copy.wait_recv()
        value = value + s["uh"][d]
    inner = jnp.sum(item_dir * value, axis=-1, keepdims=True)
    ig_ref[...] = item_inv * (value - item_dir * inner)
    for copy in started:
        copy.wait_send()


def step(sizes, query_hidden, query_proj, item_embed, positive, hard_ids):
    nx, ny, nh, nl, nc = sizes
    q, hid = query_hidden.shape
    emb, ipd = query_proj.shape[1], item_embed.shape[0]
    half, wpd = emb // 2, hid // (nx * ny * nh)
    yr, ic = nh * ipd, ny * nh * ipd
    wyr, wc = nh * wpd, ny * nh * wpd
    copies = 128
    scratch = {
        "proj": pltpu.VMEM((hid, emb), BF16),
        "item": pltpu.VMEM((ipd, emb), BF16),
        "pos": pltpu.VMEM((1, q), jnp.int32),
        "hard": pltpu.VMEM((hard_ids.shape[1], q), jnp.int32),
        "hq": pltpu.VMEM((q, hid), BF16),
        "hx": pltpu.VMEM((nx, nc * q, wc), BF16),
        "hxt": pltpu.VMEM((nx, wc, nc * q), BF16),
        "hbuf": pltpu.VMEM((nh, 2 * ipd, half), BF16),
        "hrow": pltpu.VMEM((yr, emb), F32),
        "g": pltpu.VMEM((nx, ic, emb), BF16),
        "qd": pltpu.VMEM((q, emb), F32),
        "qx": pltpu.VMEM((nx * q, emb), BF16),
        "qinv": pltpu.VMEM((q, 128), F32),
        "e": pltpu.VMEM((nx, q, ic), F32),
        "sg": pltpu.VMEM((nx, q, ic), BF16),
        "sgx": pltpu.VMEM((nx * q, ic), BF16),
        "raw": pltpu.VMEM((nc, q, half), BF16),
        "rx": pltpu.VMEM((nx, nc * q, half), BF16),
        "w_own": pltpu.VMEM((wc, half), F32),
        "w_sum": pltpu.VMEM((wc, half), BF16),
        "wy": pltpu.VMEM((ny, wyr, half), BF16),
        "wyb": pltpu.VMEM((wyr, half), BF16),
        "wz": pltpu.VMEM((nh * nl, wpd, half), BF16),
        "lc": pltpu.VMEM((nc, wpd, half), F32),
        "u_own": pltpu.VMEM((yr, emb), F32),
        "u_sum": pltpu.VMEM((ic, emb), BF16),
        "uy": pltpu.VMEM((ny, yr, emb), BF16),
        "uyf": pltpu.VMEM((yr, emb), F32),
        "uh": pltpu.VMEM((nh, ipd, emb), F32),
        "sqy": pltpu.VMEM((ny * nc, 8, 128), F32),
        "sqxh": pltpu.VMEM((nx * nh, 8, 128), F32),
        "send": pltpu.SemaphoreType.DMA((copies,)),
        "recv": pltpu.SemaphoreType.DMA((copies,)),
        "local": pltpu.SemaphoreType.DMA((6,)),
    }
    names = list(scratch)

    def body(*refs):
        kernel(sizes, *refs[:7], dict(zip(names, refs[7:])))

    vmem = pl.BlockSpec(memory_space=pltpu.VMEM)
    anywhere = pl.BlockSpec(memory_space=pltpu.HBM)
    return pl.pallas_call(
        body,
        out_shape=(
            jax.ShapeDtypeStruct((ipd, emb), F32),
            jax.ShapeDtypeStruct((wpd, emb), F32),
        ),
        in_specs=[anywhere] * 5,
        out_specs=(vmem, vmem),
        scratch_shapes=list(scratch.values()),
        compiler_params=pltpu.CompilerParams(
            collective_id=0, has_side_effects=True, vmem_limit_bytes=63 * 2**20
        ),
    )(query_hidden, query_proj, item_embed, positive.reshape(1, q), hard_ids.T)


def solution(mesh):
    return jax.shard_map(
        functools.partial(step, (NX, NY, NH, NL, NC)),
        mesh=mesh,
        in_specs=(
            P(("grp", "blk"), None),
            P(),
            P(("grp", "blk"), None),
            P(("grp", "blk")),
            P(("grp", "blk"), None),
        ),
        out_specs=(P(("grp", "blk"), None), P("blk", None)),
        check_vma=False,
    )
```
